32 devices in a mesh: batch: 8 (over z, y), head: 4 (over x, core).
Axes of the slice: x: 2, y: 2, z: 4, core: 2. Of those that a mesh axis runs over, the one named last changes fastest.
Arguments:
- frozen_input: bfloat16 [128, 128, 1024], P('batch', None, 'head'), may hold values from -6 to 6
- frozen_attend: bfloat16 [2, 3, 1024, 1024], P(None, None, None, 'head'), may hold values from -0.1875 to 0.1875
- frozen_output: bfloat16 [2, 1024, 1024], P(None, 'head'), may hold values from -0.75 to 0.75
- frozen_expand: bfloat16 [2, 1024, 4096], P(None, None, 'head'), may hold values from -0.1875 to 0.1875
- frozen_reduce: bfloat16 [2, 4096, 1024], P(None, 'head'), may hold values from -0.09375 to 0.09375
- frozen_gains: float32 [2, 2, 1024], replicated, may hold values from 0.5 to 1.5
- lengths: int32 [128, 7], P('batch'), may hold values from 20 to 128
- side_input: bfloat16 [128, 128, 128], P(('batch', 'head')), may hold values from -6 to 6
- cotangent: float32 [128, 128, 128], P(('batch', 'head')), may hold values from -12 to 12
- attend_master: float32 [1024, 128], P(('batch', 'head')), may hold values from -2 to 2
- attend_moment: float32 [1024, 128], P(('batch', 'head')), may hold values from -0.001953125 to 0.001953125
- attend_square: float32 [1024, 128], P(('batch', 'head')), may hold values from 3.8146972e-10 to 1.5258789e-09
- feed_master: float32 [512, 512], P(('batch', 'head')), may hold values from -0.5 to 0.5
- feed_moment: float32 [512, 512], P(('batch', 'head')), may hold values from -0.001953125 to 0.001953125
- feed_square: float32 [512, 512], P(('batch', 'head')), may hold values from 3.8146972e-10 to 1.5258789e-09
- down_master: float32 [2048, 128], P(('batch', 'head')), may hold values from -0.1875 to 0.1875
- down_moment: float32 [2048, 128], P(('batch', 'head')), may hold values from -0.001953125 to 0.001953125
- down_square: float32 [2048, 128], P(('batch', 'head')), may hold values from 3.8146972e-10 to 1.5258789e-09
- gains_master: float32 [6, 128], replicated, may hold values from 0.5 to 1.5
- gains_moment: float32 [6, 128], replicated, may hold values from -0.0078125 to 0.0078125
- gains_square: float32 [6, 128], replicated, may hold values from 1.5258789e-09 to 6.1035155e-09
Outputs:
- side_output: float32 [128, 128, 128], P(('batch', 'head'))
- input_grad: float32 [128, 128, 128], P(('batch', 'head'))
- grad_norm: float32 [], replicated
- attend_new: float32 [1024, 128], P(('batch', 'head'))
- attend_first: float32 [1024, 128], P(('batch', 'head'))
- attend_second: float32 [1024, 128], P(('batch', 'head'))
- attend_copy: bfloat16 [1024, 128], P(('batch', 'head'))
- feed_new: float32 [512, 512], P(('batch', 'head'))
- feed_first: float32 [512, 512], P(('batch', 'head'))
- feed_second: float32 [512, 512], P(('batch', 'head'))
- feed_copy: bfloat16 [512, 512], P(('batch', 'head'))
- down_new: float32 [2048, 128], P(('batch', 'head'))
- down_first: float32 [2048, 128], P(('batch', 'head'))
- down_second: float32 [2048, 128], P(('batch', 'head'))
- down_copy: bfloat16 [2048, 128], P(('batch', 'head'))
- gains_new: float32 [6, 128], replicated
- gains_first: float32 [6, 128], replicated
- gains_second: float32 [6, 128], replicated
The draws below stay inside these ranges and needn't reach their ends.
All inputs are finite; a program needn't handle non-finite values.
Results may differ from the reference program's by a relative error of at most 0.03.
Values may be sent and summed in bfloat16 or wider, within the bound.
No kernel may reach another device: no remote copies, remote signals or barrier semaphores. Data moves between devices by JAX's collectives and lax.ppermute only.
A program may use at most 128 MiB of HBM per device.

```python
import math
import jax
import jax.numpy as jnp
from jax import lax

D = 1024
HEAD_DIM = 64
FF = 4096
S = 128
SIDE_HD = 8
SF = 512
L = 2
ROW = 128
MAXS = 7
STEP = 10
ROWS_DEV = 4
ROWS = 128
N_BATCH = 8
N_HEAD = 4


def draw_cotangent(key, part):
    key = jax.random.fold_in(key, 11)
    sample_base = jax.random.truncated_normal(key, -4.0, 4.0, (ROWS, ROW, S), jnp.float32)
    spread = 3.0
    device_at = jnp.arange(ROWS, dtype=jnp.int32) // ROWS_DEV
    batch_at = (device_at // N_HEAD).astype(jnp.float32) / max(N_BATCH - 1, 1)
    head_at = (device_at % N_HEAD).astype(jnp.float32) / max(N_HEAD - 1, 1)
    scales = spread ** (batch_at + head_at - 1.0)
    return sample_base * scales[:, None, None]


def draw_attend_master(key, part):
    key = jax.random.fold_in(key, 12)
    sample_base = jax.random.truncated_normal(key, -4.0, 4.0, (L * 4 * S, S), jnp.float32)
    matrix_at = jnp.arange(L * 4 * S, dtype=jnp.int32) // S % 4
    scales = jnp.where(matrix_at == 3, (S // 16) ** (-0.5), S ** (-0.5))
    return sample_base * scales[:, None]


def with_ends(array, key, smallest, largest):
    longest = array.shape.index(max(array.shape))
    spots = []
    for shift in (0, 1):
        where = [jax.random.randint(jax.random.fold_in(key, axis), (), 0, length) for axis, length in enumerate(array.shape)]
        where[longest] = (where[longest] + shift) % array.shape[longest]
        spots.append(tuple(where))
    return array.at[spots[0]].set(smallest).at[spots[1]].set(largest)


def level_of(own_key, shape, shards, smallest, largest):
    factor_of = 1.0
    for position, blocks in shards:
        steps = jax.random.uniform(jax.random.fold_in(jax.random.fold_in(own_key, 6), position), (blocks,), jnp.float32, smallest / len(shards), largest / len(shards))
        factor_of = factor_of * jnp.repeat(jnp.exp(steps), shape[position] // blocks).reshape((-1,) + (1,) * (len(shape) - 1 - position))
    return factor_of


def noise(own_key, dims, width, reach, pieces=(), kind=jnp.bfloat16):
    array = jax.random.normal(own_key, dims, jnp.float32) * width
    if len(pieces) > 0:
        array = level_of(own_key, dims, pieces, -0.22, 0.18) * array
    return jnp.clip(array, min=-reach, max=reach).astype(kind)


def setup_inputs(seed: int = 0) -> dict:
    splits = jax.random.split(jax.random.key(seed), 22)
    frozen_input = noise(splits[0], (ROWS, ROW, D), 1.0, 6.0, ((0, 8), (2, 4)))
    frozen_attend = noise(splits[1], (L, 3, D, D), D ** -0.5, 0.1875, ((3, 4),))
    frozen_output = noise(splits[2], (L, D, D), (D // 16) ** -0.5, 0.75, ((1, 4),))
    frozen_expand = noise(splits[3], (L, D, FF), D ** -0.5, 0.1875, ((2, 4),))
    frozen_reduce = noise(splits[4], (L, FF, D), FF ** -0.5, 0.09375, ((1, 4),))
    frozen_gains = jnp.clip(1.0 + 0.1 * jax.random.normal(splits[5], (L, 2, D), jnp.float32), 0.5, 1.5)
    lengths = with_ends(jax.random.randint(splits[6], (ROWS, MAXS), ROW * 5 // 32, ROW + 1), jax.random.fold_in(splits[6], 1), ROW * 5 // 32, ROW).astype(jnp.int32)
    side_input = noise(splits[7], (ROWS, ROW, S), 1.0, 6.0, ((0, 32),))
    cotangent = draw_cotangent(jax.random.fold_in(splits[21], 71), 0)
    attend_master = draw_attend_master(jax.random.fold_in(splits[21], 71), 0)
    attend_moment = noise(splits[10], (L * 4 * S, S), (0.111 * (L * (4 * S * S + 2 * S * SF + D * S)) ** -0.5), 0.001953125, ((0, 32),), jnp.float32)
    attend_square = jnp.clip(jnp.exp(math.log(1.5258788677030566e-09) - 1.3862944 * jax.random.uniform(splits[11], (L * 4 * S, S), jnp.float32) ** level_of(splits[11], (L * 4 * S, S), ((0, 32),), -0.2, 0.2)), 3.8146971692576415e-10, 1.5258788677030566e-09)
    feed_master = noise(splits[12], (L * 2 * S, SF), S ** -0.5, 0.5, ((0, 32),), jnp.float32)
    feed_moment = noise(splits[13], (L * 2 * S, SF), (0.111 * (L * (4 * S * S + 2 * S * SF + D * S)) ** -0.5), 0.001953125, ((0, 32),), jnp.float32)
    feed_square = jnp.clip(jnp.exp(math.log(1.5258788677030566e-09) - 1.3862944 * jax.random.uniform(splits[14], (L * 2 * S, SF), jnp.float32) ** level_of(splits[14], (L * 2 * S, SF), ((0, 32),), -0.2, 0.2)), 3.8146971692576415e-10, 1.5258788677030566e-09)
    down_master = noise(splits[15], (L * D, S), D ** -0.5, 0.1875, ((0, 32),), jnp.float32)
    down_moment = noise(splits[16], (L * D, S), (0.111 * (L * (4 * S * S + 2 * S * SF + D * S)) ** -0.5), 0.001953125, ((0, 32),), jnp.float32)
    down_square = jnp.clip(jnp.exp(math.log(1.5258788677030566e-09) - 1.3862944 * jax.random.uniform(splits[17], (L * D, S), jnp.float32) ** level_of(splits[17], (L * D, S), ((0, 32),), -0.2, 0.2)), 3.8146971692576415e-10, 1.5258788677030566e-09)
    gains_master = jnp.clip(jax.random.uniform(splits[18], (L * 3, S), jnp.float32, 0.5, 1.5), 0.5, 1.5)
    gains_moment = noise(splits[19], (L * 3, S), (0.444 * (L * (4 * S * S + 2 * S * SF + D * S)) ** -0.5), 0.0078125, (), jnp.float32)
    gains_square = jnp.clip(jnp.exp(jax.random.uniform(splits[20], (L * 3, S), jnp.float32, math.log(1.5258788677030566e-09), math.log(6.103515470812226e-09))), 1.5258788677030566e-09, 6.103515470812226e-09)
    return dict(frozen_input=frozen_input, frozen_attend=frozen_attend, frozen_output=frozen_output, frozen_expand=frozen_expand, frozen_reduce=frozen_reduce, frozen_gains=frozen_gains, lengths=lengths, side_input=side_input, cotangent=cotangent, attend_master=attend_master, attend_moment=attend_moment, attend_square=attend_square, feed_master=feed_master, feed_moment=feed_moment, feed_square=feed_square, down_master=down_master, down_moment=down_moment, down_square=down_square, gains_master=gains_master, gains_moment=gains_moment, gains_square=gains_square)


NORM_EPS = 1e-06
THRESHOLD = 1.0
BETA_ONE = 0.9
BETA_TWO = 0.999
ADAM_EPS = 1e-08
RATE_MATRIX = 0.12
RATE_SMALL = 0.5
WEIGHT_DECAY = 0.01
MASKED = -1e+30
PRECISE = lax.Precision.HIGHEST

@jax.custom_vjp
def low(v):
    return lax.optimization_barrier(v.astype(jnp.bfloat16)).astype(jnp.float32)

@jax.custom_vjp
def low_back(v):
    return v

def low_keep(v):
    return (low(v), None)

def low_pass(kept, grad):
    return (grad,)

def back_keep(v):
    return (v, None)

def back_low(kept, grad):
    return (low(grad),)
low.defvjp(low_keep, low_pass)
low_back.defvjp(back_keep, back_low)

def root_norm(values, gains):
    return values * lax.rsqrt(lax.optimization_barrier(jnp.mean(values * values, axis=-1, keepdims=True)) + NORM_EPS) * gains

def segments(lengths):
    sent_ends = jnp.cumsum(lengths, axis=-1)
    kept_flag = sent_ends <= ROW
    places = jnp.arange(ROW, dtype=jnp.int32)
    labels = lax.optimization_barrier(jnp.sum((kept_flag[:, None, :] & (sent_ends[:, None, :] <= places[None, :, None])).astype(jnp.int32), axis=-1))
    filled = lax.optimization_barrier(jnp.sum(jnp.where(kept_flag, lengths, 0), axis=-1))
    real_tok = (places[None, :] < filled[:, None]).astype(jnp.float32)
    return (labels[:, :, None] == labels[:, None, :], real_tok)

def backbone_attention(normed, w_attend, same_seg):
    col_count = w_attend.shape[2]
    projected = low(jnp.einsum('rtd,jdc->jrtc', normed, w_attend, precision=PRECISE))
    head_shape = normed.shape[:2] + (col_count // HEAD_DIM, HEAD_DIM)
    queries = projected[0].reshape(head_shape)
    key_rows = projected[1].reshape(head_shape)
    value_rows = projected[2].reshape(head_shape)
    scores = jnp.einsum('rqhc,rkhc->rhqk', queries, key_rows, precision=PRECISE) * HEAD_DIM ** (-0.5)
    scores = jnp.where(same_seg[:, None], scores, MASKED)
    shares = low(jax.nn.softmax(scores, axis=-1))
    context = low(jnp.einsum('rhqk,rkhc->rqhc', shares, value_rows, precision=PRECISE))
    return context.reshape(normed.shape[:2] + (col_count,))

def backbone_layer(hidden, w_attend, w_output, w_expand, w_reduce, gains, same_seg):
    normed = low(root_norm(hidden, gains[0]))
    context = backbone_attention(normed, w_attend, same_seg)
    hidden = low(hidden + jnp.einsum('rtc,cd->rtd', context, w_output, precision=PRECISE))
    normed = low(root_norm(hidden, gains[1]))
    inner = low(jax.nn.gelu(jnp.einsum('rtd,df->rtf', normed, w_expand, precision=PRECISE)))
    return low(hidden + jnp.einsum('rtf,fd->rtd', inner, w_reduce, precision=PRECISE))

def side_forward(attend_w, feed_w, down_w, gains_w, side_state, taps, same_seg):
    mats_all = attend_w.reshape(L, 4, S, S)
    feeds_all = feed_w.reshape(L, 2, S, SF)
    downs = down_w.reshape(L, D, S)
    smalls_all = gains_w.reshape(L, 3, S)
    head_shape = side_state.shape[:2] + (S // SIDE_HD, SIDE_HD)
    for layer_at in range(L):
        mats = low(mats_all[layer_at])
        feeds = low(feeds_all[layer_at])
        smalls = smalls_all[layer_at]
        tapped = low_back(jnp.einsum('rtd,ds->rts', taps[layer_at], low(downs[layer_at]), precision=PRECISE))
        gating = jax.nn.sigmoid(smalls[2])
        mixed = gating * tapped + (1.0 - gating) * side_state
        normed = low(root_norm(mixed, smalls[0]))
        projected = low(low_back(jnp.einsum('rts,jsc->jrtc', normed, mats[:3], precision=PRECISE)))
        queries = projected[0].reshape(head_shape)
        key_rows = projected[1].reshape(head_shape)
        value_rows = projected[2].reshape(head_shape)
        scores = low_back(jnp.einsum('rqhc,rkhc->rhqk', queries, key_rows, precision=PRECISE) * SIDE_HD ** (-0.5))
        scores = jnp.where(same_seg[:, None], scores, MASKED)
        shares = low(jax.nn.softmax(scores, axis=-1))
        context = low(low_back(jnp.einsum('rhqk,rkhc->rqhc', shares, value_rows, precision=PRECISE))).reshape(side_state.shape)
        middle = mixed + low_back(jnp.einsum('rtc,cs->rts', context, mats[3], precision=PRECISE))
        normed_two = low(root_norm(middle, smalls[1]))
        inner = low_back(jnp.einsum('rts,sf->rtf', normed_two, feeds[0], precision=PRECISE))
        active = low(jax.nn.gelu(inner))
        side_state = middle + low_back(jnp.einsum('rtf,sf->rts', active, feeds[1], precision=PRECISE))
    return side_state

def adamw(master, moment, square, grad_now, clip, rate, decay):
    grad_now = grad_now * clip
    moment = BETA_ONE * moment + (1.0 - BETA_ONE) * grad_now
    square = BETA_TWO * square + (1.0 - BETA_TWO) * grad_now * grad_now
    first_hat = moment / (1.0 - BETA_ONE ** STEP)
    second_hat = square / (1.0 - BETA_TWO ** STEP)
    master = master - rate * (first_hat / (jnp.sqrt(second_hat) + ADAM_EPS) + decay * master)
    return (master, moment, square)

def reference(frozen_input, frozen_attend, frozen_output, frozen_expand, frozen_reduce, frozen_gains, lengths, side_input, cotangent, attend_master, attend_moment, attend_square, feed_master, feed_moment, feed_square, down_master, down_moment, down_square, gains_master, gains_moment, gains_square):
    group_rows = ROWS // N_BATCH
    masters = (attend_master, feed_master, down_master, gains_master)
    w_attend = frozen_attend.astype(jnp.float32)
    w_output = frozen_output.astype(jnp.float32)
    w_expand = frozen_expand.astype(jnp.float32)
    w_reduce = frozen_reduce.astype(jnp.float32)

    def one_group(totals, inputs):
        rows_in, lengths_in, side_in, cot_in = inputs
        same_seg, real_tok = segments(lengths_in)
        hidden = rows_in.astype(jnp.float32)
        taps = []
        for layer_at in range(L):
            hidden = backbone_layer(hidden, w_attend[layer_at], w_output[layer_at], w_expand[layer_at], w_reduce[layer_at], frozen_gains[layer_at], same_seg)
            taps.append(hidden)

        def forward(attend_w, feed_w, down_w, gains_w, side_state):
            return side_forward(attend_w, feed_w, down_w, gains_w, side_state, taps, same_seg)
        result, backward = jax.vjp(forward, *masters, side_in.astype(jnp.float32))
        grads = backward(cot_in * real_tok[:, :, None])
        totals = tuple((tally + fresh for tally, fresh in zip(totals, grads[:4])))
        return (totals, (result, grads[4]))
    inputs = (frozen_input.reshape(N_BATCH, group_rows, ROW, D), lengths.reshape(N_BATCH, group_rows, MAXS), side_input.reshape(N_BATCH, group_rows, ROW, S), cotangent.reshape(N_BATCH, group_rows, ROW, S))
    start = tuple((jnp.zeros(master.shape, jnp.float32) for master in masters))
    totals, (outputs, input_grads) = lax.scan(one_group, start, inputs)
    squares = jnp.sum(totals[0] * totals[0]) + jnp.sum(totals[1] * totals[1]) + jnp.sum(totals[2] * totals[2]) + jnp.sum(totals[3] * totals[3])
    grad_norm = jnp.sqrt(squares)
    clip = jnp.minimum(1.0, THRESHOLD / grad_norm)
    attend_new, attend_first, attend_second = adamw(attend_master, attend_moment, attend_square, totals[0], clip, RATE_MATRIX, WEIGHT_DECAY)
    feed_new, feed_first, feed_second = adamw(feed_master, feed_moment, feed_square, totals[1], clip, RATE_MATRIX, WEIGHT_DECAY)
    down_new, down_first, down_second = adamw(down_master, down_moment, down_square, totals[2], clip, RATE_MATRIX, WEIGHT_DECAY)
    gains_new, gains_first, gains_second = adamw(gains_master, gains_moment, gains_square, totals[3], clip, RATE_SMALL, 0.0)
    return (outputs.reshape(ROWS, ROW, S), input_grads.reshape(ROWS, ROW, S), grad_norm, attend_new, attend_first, attend_second, attend_new.astype(jnp.bfloat16), feed_new, feed_first, feed_second, feed_new.astype(jnp.bfloat16), down_new, down_first, down_second, down_new.astype(jnp.bfloat16), gains_new, gains_first, gains_second)
```

```python
from functools import partial

import jax
import jax.numpy as jnp
from jax import lax
from jax.experimental import pallas as pl
from jax.experimental.pallas import tpu as pltpu
from jax.sharding import PartitionSpec as P

D = 1024
HEAD_DIM = 64
S = 128
SIDE_HD = 8
SF = 512
L = 2
ROW = 128
STEP = 10


NORM_EPS = 1e-06
THRESHOLD = 1.0
BETA_ONE = 0.9
BETA_TWO = 0.999
ADAM_EPS = 1e-08
RATE_MATRIX = 0.12
RATE_SMALL = 0.5
WEIGHT_DECAY = 0.01
MASKED = -1e30

BF = jnp.bfloat16
F32 = jnp.float32
BLK = 256
PLACES = 32
MIB = 2**20

VM = pl.BlockSpec(memory_space=pltpu.VMEM)
SM = pl.BlockSpec(memory_space=pltpu.SMEM)
HB = pl.BlockSpec(memory_space=pltpu.HBM)


def shape_of(dims, kind):
    return jax.ShapeDtypeStruct(dims, kind)


def params(mib):
    return pltpu.CompilerParams(vmem_limit_bytes=mib * MIB)


def cost(micros):
    return pl.CostEstimate(flops=int(micros * 4e9), bytes_accessed=0, transcendentals=0)


def gelu(values):
    squared = values * values
    half = 0.5 * values
    bent = jnp.tanh(values * (0.7978845608028654 + 0.7978845608028654 * 0.044715 * squared))
    return half + half * bent


class Fetch:
    def __init__(self, sems):
        self.sems, self.items = sems, []

    def start(self, source, target):
        item = pltpu.make_async_copy(source, target, self.sems.at[len(self.items)])
        self.items.append(item)
        item.start()
        return item


def nn(a, b):
    return lax.dot_general(a, b, (((1,), (0,)), ((), ())), preferred_element_type=F32)


def nt(a, b):
    return lax.dot_general(a, b, (((1,), (1,)), ((), ())), preferred_element_type=F32)


def norm_scale(values):
    return lax.rsqrt(jnp.mean(values * values, axis=-1, keepdims=True) + NORM_EPS)


def root_norm(values, gains):
    return values * norm_scale(values) * gains


def segments(lengths):
    sent_ends = jnp.cumsum(lengths, axis=-1)
    kept_flag = sent_ends <= ROW
    places = jnp.arange(ROW, dtype=jnp.int32)
    labels = jnp.sum(
        (kept_flag[:, None, :] & (sent_ends[:, None, :] <= places[None, :, None])).astype(
            jnp.int32
        ),
        axis=-1,
    )
    filled = jnp.sum(jnp.where(kept_flag, lengths, 0), axis=-1)
    real_tok = (places[None, :] < filled[:, None]).astype(jnp.float32)
    return (labels[:, :, None] == labels[:, None, :], real_tok)


def side_by_side(rows2):
    return jnp.concatenate([rows2[:ROW], rows2[ROW:]], axis=1)


def block_diagonal(rows2):
    blank = jnp.zeros((ROW, ROW), rows2.dtype)
    top = jnp.concatenate([rows2[:ROW], blank], axis=1)
    low = jnp.concatenate([blank, rows2[ROW:]], axis=1)
    return jnp.concatenate([top, low], axis=0)


def head_masks(head_dim, first):
    lanes = lax.broadcasted_iota(jnp.int32, (ROW, 2 * ROW), 1) % ROW // head_dim
    return (lanes == first, lanes == first + 1)


def stack_heads(wide, masks):
    blank = jnp.zeros_like(wide)
    return jnp.concatenate(
        [jnp.where(masks[0], wide, blank), jnp.where(masks[1], wide, blank)], axis=0
    )


def pair_shares(key_stack, query_diag, bias, scale):
    scores = nt(key_stack, query_diag)
    if scale is not None:
        scores = scores * scale
    scores = scores.reshape(2, ROW, 2 * ROW) + bias[None]
    highest = jnp.max(scores, axis=1, keepdims=True)
    weights = jnp.exp(scores - highest)
    return weights * (1.0 / jnp.sum(weights, axis=1, keepdims=True))


def head_rows(flipped, count):
    rows = lax.broadcasted_iota(jnp.int32, flipped.shape, 0)
    blank = jnp.zeros_like(flipped)
    return jnp.concatenate(
        [jnp.where(rows < count, flipped, blank), jnp.where(rows >= count, flipped, blank)], axis=1
    )


def unrolled(count, step, width=2):
    def some(turn, carry):
        for at in range(width):
            step(turn * width + at)
        return carry

    lax.fori_loop(0, count // width, some, 0)


def flip(values):
    return values.astype(F32).T


def backbone_heads(proj, bias_ref, context_ref):
    masks = head_masks(HEAD_DIM, 0)
    for pair in range(proj.shape[1] // (2 * ROW)):
        rows = slice(pair * 2 * ROW, (pair + 1) * 2 * ROW)
        bias = bias_ref[pair]
        for lane_at in range(proj.shape[2] // ROW):
            lanes = slice(lane_at * ROW, (lane_at + 1) * ROW)
            queries = proj[0, rows, lanes] * jnp.asarray(HEAD_DIM**-0.5, BF)
            keys = proj[1, rows, lanes]
            values = proj[2, rows, lanes]
            shares = pair_shares(
                stack_heads(side_by_side(keys), masks), block_diagonal(queries), bias, None
            )
            shares = shares.astype(BF).reshape(2 * ROW, 2 * ROW)
            for at in range(2):
                flipped = flip(values[at * ROW : (at + 1) * ROW]).astype(BF)
                out = nn(head_rows(flipped, HEAD_DIM), shares[:, at * ROW : (at + 1) * ROW])
                start = pair * 2 * ROW + at * ROW
                context_ref[start : start + ROW, lanes] = out.T.astype(BF)


def assemble_kernel(place, own, near, far, far_near, gains, hidden_ref, normed_ref, other_ref):
    rows = own.shape[0] // 2
    whole = (hidden_ref, other_ref)
    for core, target in enumerate(whole):
        mine = pl.ds((place[2] ^ core) * rows, rows)
        for step, piece in enumerate((own, near, far, far_near)):
            spot = pl.multiple_of((place[0] ^ step) * BLK, BLK)
            target[:, pl.ds(spot, BLK)] = piece[mine].reshape(rows * ROW, BLK)
    for source, target in zip(whole, (normed_ref, other_ref)):
        target[...] = root_norm(source[...].astype(F32), gains[0, 0:1]).astype(BF)


def attend_kernel(layer, normed, weights, bias, context, proj, held, sems):
    fetch = Fetch(sems)
    waits = [fetch.start(weights.at[layer, at], held.at[at]) for at in range(3)]
    for at in range(3):
        waits[at].wait()
        proj[at] = nn(normed[...], held[at]).astype(BF)
    backbone_heads(proj, bias, context)


def attend_far_kernel(layer, place, normed, bias, context_own, out, *rest):
    parts, (total, proj, context, turned, held, sems) = rest[:4], rest[4:]
    fetch = Fetch(sems)
    wait = fetch.start(out.at[layer], held)
    spots = [pl.ds(pl.multiple_of((place[1] ^ step) * BLK, BLK), BLK) for step in range(4)]
    for step, spot in enumerate(spots):
        turned[:, step * BLK : (step + 1) * BLK] = normed[:, spot]
    for at in range(3):
        weights = jnp.concatenate([part[at] for part in parts], axis=0)
        proj[at] = nn(turned[...], weights).astype(BF)
    backbone_heads(proj, bias, context)
    wait.wait()
    both = jnp.concatenate([context_own[...], context[...]], axis=1)
    for step, spot in enumerate(spots):
        weights = jnp.concatenate([held[:, spot], parts[step][3]], axis=0)
        total[:, spot] = nn(both, weights).astype(total.dtype)


def finish_kernel(gain_at, hidden, total, came, gains, *outs):
    value = hidden[...].astype(F32) + (total[...] + came[...].astype(F32))
    value = value.astype(BF)
    outs[0][...] = value
    if gain_at is not None:
        layer, at = gain_at
        outs[1][...] = root_norm(value.astype(F32), gains[layer, at : at + 1]).astype(BF)


def feed_kernel(layer, normed, expand, reduce, total_ref, wide, tall, sems):
    fetch = Fetch(sems)
    waits = []
    for at in range(expand.shape[2] // (2 * BLK)):
        units = pl.ds(at * 2 * BLK, 2 * BLK)
        waits.append(
            (
                fetch.start(expand.at[layer, :, units], wide.at[at]),
                fetch.start(reduce.at[layer, units, :], tall.at[at]),
            )
        )
    for at, (expand_wait, reduce_wait) in enumerate(waits):
        expand_wait.wait()
        inner = gelu(nn(normed[...], wide[at])).astype(BF)
        reduce_wait.wait()
        term = nn(inner, tall[at])
        if at == 0:
            total_ref[...] = term
        else:
            total_ref[...] += term


def feed_far_kernel(count, sets, *refs):
    normed, totals = refs[:sets], refs[sets : 2 * sets]
    parts, outs = refs[2 * sets : 2 * sets + count], refs[2 * sets + count :]
    for values, total, out in zip(normed, totals, outs):
        inners = [gelu(nn(values[...], part[0:4].reshape(D, BLK))).astype(BF) for part in parts]
        inner = jnp.concatenate(inners, axis=1)
        for at in range(4):
            weights = jnp.concatenate([part[4 + at] for part in parts], axis=0)
            columns = slice(at * BLK, (at + 1) * BLK)
            out[:, columns] = (total[:, columns] + nn(inner, weights)).astype(out.dtype)


def pack_first_kernel(place, hidden, attend, output, chip_far, chip_own, attend_part, sems):
    fetch = Fetch(sems)
    spot = pl.ds(pl.multiple_of(place[1] * BLK, BLK), BLK)
    for at in range(3):
        fetch.start(attend.at[0, at, spot, :], attend_part.at[at])
    fetch.start(output.at[0, :, spot], attend_part.at[3])
    rows = chip_own.shape[0]
    fetch.start(hidden.at[pl.ds((1 - place[3]) * rows, rows)], chip_far)
    fetch.start(hidden.at[pl.ds(place[3] * rows, rows)], chip_own)
    for item in fetch.items:
        item.wait()


def pack_first(place, hidden, attend, output):
    half = (hidden.shape[0] // 2,) + hidden.shape[1:]
    return pl.pallas_call(
        pack_first_kernel,
        out_shape=[shape_of(half, BF)] * 2 + [shape_of((4, BLK, BLK), BF)],
        in_specs=[SM] + [HB] * 3,
        out_specs=[VM] * 3,
        scratch_shapes=[pltpu.SemaphoreType.DMA((6,))],
        compiler_params=params(57),
        cost_estimate=cost(1.0),
    )(place, hidden, attend, output)


def pack_kernel(place, attend, output, expand, reduce, attend_part, *rest):
    feed_targets, sems = rest[:-1], rest[-1]
    fetch = Fetch(sems)
    spot = pl.ds(pl.multiple_of(place[1] * BLK, BLK), BLK)
    last = pl.ds(pl.multiple_of((place[1] ^ 3) * BLK, BLK), BLK)
    for layer, units, target in zip((0, 1, 1), (spot, spot, last), feed_targets):
        for at in range(4):
            rows = pl.ds(at * BLK, BLK)
            fetch.start(expand.at[layer, rows, units], target.at[at])
            fetch.start(reduce.at[layer, units, rows], target.at[4 + at])
    for at in range(3):
        fetch.start(attend.at[1, at, spot, :], attend_part.at[at])
    fetch.start(output.at[1, :, spot], attend_part.at[3])
    for item in fetch.items:
        item.wait()


def pack(place, attend, output, expand, reduce):
    return pl.pallas_call(
        pack_kernel,
        out_shape=[shape_of((4, BLK, BLK), BF)] + [shape_of((8, BLK, BLK), BF)] * 3,
        in_specs=[SM] + [HB] * 4,
        out_specs=[VM] * 4,
        scratch_shapes=[pltpu.SemaphoreType.DMA((28,))],
        compiler_params=params(57),
        cost_estimate=cost(2.0),
    )(place, attend, output, expand, reduce)


def prepare_kernel(lengths, place, cotangent, *rest):
    masters, (bias_ref, other_ref, seed_ref, *packed) = rest[:3], rest[3:]
    rows = cotangent.shape[0] // ROW
    deep = lax.broadcasted_iota(jnp.int32, (ROW, ROW), 0)
    across = lax.broadcasted_iota(jnp.int32, (ROW, ROW), 1)
    for row in range(2 * rows):
        core, row = row // rows, row % rows
        end = jnp.int32(0)
        filled = jnp.int32(0)
        deep_label = jnp.zeros((ROW, ROW), jnp.int32)
        across_label = jnp.zeros((ROW, ROW), jnp.int32)
        for slot in range(lengths.shape[1]):
            length = lengths[(place[0] ^ core) * rows + row, slot]
            end = end + length
            kept = end <= ROW
            filled = filled + jnp.where(kept, length, 0)
            start = jnp.where(kept, end, ROW)
            deep_label += (deep >= start).astype(jnp.int32)
            across_label += (across >= start).astype(jnp.int32)
        pair, at = row // 2, row % 2
        target = other_ref if core else bias_ref
        target[pair, :, at * ROW : (at + 1) * ROW] = jnp.where(
            deep_label == across_label, 0.0, MASKED
        )
        if core:
            continue
        spot = slice(row * ROW, (row + 1) * ROW)
        seed_ref[spot] = jnp.where(deep < filled, cotangent[spot], 0.0)
    if packed:
        base = 0
        for master in masters:
            height, width = master.shape
            for column in range(width // S):
                packed[0][0, base : base + height] = master[:, column * S : (column + 1) * S].astype(BF)
                base += height


def prepare(lengths, place, cotangent, masters, packed):
    tokens = cotangent.shape[0]
    shapes = [shape_of((tokens // ROW // 2, ROW, 2 * ROW), F32)] * 2 + [shape_of((tokens, S), F32)]
    if packed:
        shapes.append(shape_of((1, sum(master.size for master in masters) // S, S), BF))
    return pl.pallas_call(
        prepare_kernel,
        out_shape=shapes,
        in_specs=[SM, SM] + [VM] * 4,
        out_specs=[VM] * len(shapes),
        compiler_params=params(8),
        cost_estimate=cost(1.5),
    )(lengths, place, cotangent, *masters)


SAVED = (
    ("tapped", F32),
    ("mixed", F32),
    ("middle", F32),
    ("queries", BF),
    ("keys", BF),
    ("values", BF),
    ("context", BF),
)


def gathered_at(device):
    order = (1, 2, 3, 4, 0)
    return sum((device >> bit & 1) << at for at, bit in enumerate(order))


def matrix_loader(place, whole, places):
    heights = (L * 4 * S // places, L * 2 * S // places, L * D // places)
    feed_base = heights[0]
    down_base = feed_base + heights[1] * (SF // S)

    def rows(first, total, base, height):
        start = first // height
        return jnp.concatenate(
            [
                whole[gathered_at(start + step) ^ place[9], base : base + height]
                for step in range(total // height)
            ],
            axis=0,
        )

    def load(layer, mats, feeds, down=None):
        for at in range(4):
            mats[at] = rows((layer * 4 + at) * S, S, 0, heights[0])
        for at in range(2):
            for column in range(SF // S):
                feeds[at, :, column * S : (column + 1) * S] = rows(
                    (layer * 2 + at) * S, S, feed_base + column * heights[1], heights[1]
                )
        if down is not None:
            down[...] = rows(layer * D, D, down_base, heights[2])

    return load


def side_forward(tap_source, down, state, mats, feeds, smalls, bias_ref, saved, flips, result_ref):
    tokens = state.shape[0]
    gating = jax.nn.sigmoid(smalls[2:3])
    tapped = nn(tap_source, down)
    mixed = gating * tapped + (1.0 - gating) * state
    saved["tapped"][...] = tapped
    saved["mixed"][...] = mixed
    normed = (mixed * norm_scale(mixed) * smalls[0:1]).astype(BF)
    for at, name in enumerate(("queries", "keys", "values")):
        saved[name][...] = nn(normed, mats[at]).astype(BF)
    for at in range(tokens // ROW):
        flips[0, at] = flip(saved["values"][at * ROW : (at + 1) * ROW]).astype(BF)
    pairs = tokens // (2 * ROW)
    heads = S // SIDE_HD // 2

    def step(turn):
        pair, head = turn // heads, turn % heads
        rows = pl.ds(pl.multiple_of(pair * 2 * ROW, 2 * ROW), 2 * ROW)
        masks = head_masks(SIDE_HD, 2 * head)
        shares = pair_shares(
            stack_heads(side_by_side(saved["keys"][rows]), masks),
            block_diagonal(saved["queries"][rows]),
            bias_ref[pair],
            SIDE_HD**-0.5,
        )
        shares = shares.astype(BF).reshape(2 * ROW, 2 * ROW)
        spot = pl.ds(pl.multiple_of(head * 2 * SIDE_HD, 2 * SIDE_HD), 2 * SIDE_HD)
        for at in range(2):
            lhs = head_rows(flips[0, 2 * pair + at, spot], SIDE_HD)
            flips[1, 2 * pair + at, spot] = nn(lhs, shares[:, at * ROW : (at + 1) * ROW]).astype(
                BF
            )

    unrolled(pairs * heads, step)
    for at in range(tokens // ROW):
        saved["context"][at * ROW : (at + 1) * ROW] = flip(flips[1, at]).astype(BF)
    middle = mixed + nn(saved["context"][...], mats[3])
    saved["middle"][...] = middle
    normed_two = (middle * norm_scale(middle) * smalls[1:2]).astype(BF)
    active = gelu(nn(normed_two, feeds[0])).astype(BF)
    result_ref[...] = middle + nt(active, feeds[1])


def gelu_parts(inner):
    root = 0.7978845608028654
    squared = inner * inner
    bent = jnp.tanh(root * inner * (1.0 + 0.044715 * squared))
    half = 0.5 * (1.0 + bent)
    slope = half + 0.5 * inner * (1.0 - bent * bent) * (root * (1.0 + 3.0 * 0.044715 * squared))
    return (inner * half, slope)


def norm_back(values, scale, gains, grad_normed):
    weighted = grad_normed * gains
    grad_values = scale * weighted - values * scale**3 * jnp.mean(
        weighted * values, axis=-1, keepdims=True
    )
    return (grad_values, jnp.sum(grad_normed * values * scale, axis=0, keepdims=True))


def side_backward(tap_source, state, grad_out, mats, feeds, smalls, bias_ref, saved, work, put):
    flips, grads, grad_flips = work
    tokens = grad_out.shape[0]
    pairs = tokens // (2 * ROW)
    heads = S // SIDE_HD // 2
    middle = saved["middle"][...]
    second_scale = norm_scale(middle)
    normed_two = (middle * second_scale * smalls[1:2]).astype(BF)
    active, slope = gelu_parts(nn(normed_two, feeds[0]))
    grad_outer = grad_out.astype(BF)
    put("feed", 1, nn(flip(grad_outer).astype(BF), active.astype(BF)))
    grad_inner = (nn(grad_outer, feeds[1]) * slope).astype(BF)
    put("feed", 0, nn(flip(normed_two).astype(BF), grad_inner))
    grad_middle, grad_gain_two = norm_back(
        middle, second_scale, smalls[1:2], nt(grad_inner, feeds[0])
    )
    put("gain", 1, grad_gain_two)
    grad_middle = grad_middle + grad_out
    grad_branch = grad_middle.astype(BF)
    put("attend", 3, nn(flip(saved["context"][...]).astype(BF), grad_branch))
    grads[0] = nt(grad_branch, mats[3]).astype(BF).astype(F32)
    grads[1] = jnp.zeros_like(grads[1])
    grads[2] = jnp.zeros_like(grads[2])
    for at in range(tokens // ROW):
        flips[0, at] = flip(saved["keys"][at * ROW : (at + 1) * ROW]).astype(BF)

    def step(turn):
        pair, head = turn // heads, turn % heads
        rows = pl.ds(pl.multiple_of(pair * 2 * ROW, 2 * ROW), 2 * ROW)
        masks = head_masks(SIDE_HD, 2 * head)
        query_diag = block_diagonal(saved["queries"][rows])
        context_diag = block_diagonal(grads[0, rows].astype(BF))
        shares = pair_shares(
            stack_heads(side_by_side(saved["keys"][rows]), masks),
            query_diag,
            bias_ref[pair],
            SIDE_HD**-0.5,
        )
        grad_shares = nt(stack_heads(side_by_side(saved["values"][rows]), masks), context_diag)
        grad_shares = grad_shares.reshape(2, ROW, 2 * ROW)
        mean = jnp.sum(shares * grad_shares, axis=1, keepdims=True)
        grad_scores = (shares * (grad_shares - mean)).astype(BF).reshape(2 * ROW, 2 * ROW)
        shares = shares.astype(BF).reshape(2 * ROW, 2 * ROW)
        for slot, left, right in ((2, shares, context_diag), (1, grad_scores, query_diag)):
            whole = nn(left, right)
            blank = jnp.zeros((ROW, 2 * ROW), F32)
            picked = jnp.where(masks[0], whole[:ROW], blank) + jnp.where(
                masks[1], whole[ROW:], blank
            )
            first = pl.ds(pl.multiple_of(pair * 2 * ROW, 2 * ROW), ROW)
            second = pl.ds(pl.multiple_of(pair * 2 * ROW + ROW, ROW), ROW)
            grads[slot, first] += picked[:, :ROW]
            grads[slot, second] += picked[:, ROW:]
        spot = pl.ds(pl.multiple_of(head * 2 * SIDE_HD, 2 * SIDE_HD), 2 * SIDE_HD)
        for at in range(2):
            lhs = head_rows(flips[0, 2 * pair + at, spot], SIDE_HD)
            grad_flips[2 * pair + at, spot] = nn(lhs, grad_scores[:, at * ROW : (at + 1) * ROW])

    unrolled(pairs * heads, step)
    for at in range(tokens // ROW):
        grads[0, at * ROW : (at + 1) * ROW] = grad_flips[at].T
    root = SIDE_HD**-0.5
    mixed = saved["mixed"][...]
    first_scale = norm_scale(mixed)
    normed_flip = flip((mixed * first_scale * smalls[0:1]).astype(BF)).astype(BF)
    grad_normed = None
    for at, factor in enumerate((root, root, None)):
        grad = grads[at] if factor is None else grads[at] * factor
        grad = grad.astype(BF)
        put("attend", at, nn(normed_flip, grad))
        term = nt(grad, mats[at])
        grad_normed = term if grad_normed is None else grad_normed + term
    grad_mixed, grad_gain_one = norm_back(mixed, first_scale, smalls[0:1], grad_normed)
    put("gain", 0, grad_gain_one)
    grad_mixed = grad_mixed + grad_middle
    gating = jax.nn.sigmoid(smalls[2:3])
    grad_tap = (gating * grad_mixed).astype(BF)
    put(
        "gain",
        2,
        jnp.sum(grad_mixed * (saved["tapped"][...] - state), axis=0, keepdims=True)
        * gating
        * (1.0 - gating),
    )
    put("down", 0, nn(flip(grad_tap).astype(BF), tap_source).T)
    return (1.0 - gating) * grad_mixed


MATRICES = [
    pltpu.VMEM((4, S, S), BF),
    pltpu.VMEM((2, S, SF), BF),
    pltpu.VMEM((D, S), BF),
]


def side_first_kernel(place, tap_source, whole, state, smalls, bias, *rest):
    outs, (flips, mats, feeds, down) = rest[:-4], rest[-4:]
    matrix_loader(place, whole, PLACES)(0, mats, feeds, down)
    saved = {name: ref for (name, _), ref in zip(SAVED, outs)}
    side_forward(
        tap_source[...],
        down[...],
        state[...].astype(F32),
        mats,
        feeds,
        smalls[0:3],
        bias,
        saved,
        flips,
        outs[-1],
    )


def side_first(place, tap_source, whole, state, smalls, bias):
    tokens = state.shape[0]
    return pl.pallas_call(
        side_first_kernel,
        out_shape=[shape_of((tokens, S), kind) for _, kind in SAVED]
        + [shape_of((tokens, S), F32)],
        in_specs=[SM] + [VM] * 5,
        out_specs=[VM] * (len(SAVED) + 1),
        scratch_shapes=[pltpu.VMEM((2, tokens // ROW, S, ROW), BF)] + MATRICES,
        compiler_params=params(16),
        cost_estimate=cost(8.0),
    )(place, tap_source, whole, state, smalls, bias)


def side_last_kernel(
    packed,
    place,
    tap_one,
    tap_two,
    whole_in,
    state_in,
    state,
    cotangent,
    smalls,
    bias,
    *rest,
):
    count = len(SAVED)
    saved_one = {name: ref for (name, _), ref in zip(SAVED, rest[:count])}
    rest = rest[count:]
    result_ref, grad_ref = rest[:2]
    outs = rest[2:4] if packed else rest[2:6]
    rest = rest[len(outs) + 2 :]
    saved_two = {name: ref for (name, _), ref in zip(SAVED, rest[:count])}
    flips, grads, grad_flips, mats, feeds, down = rest[count : count + 6]
    load = matrix_loader(place, whole_in, PLACES)
    load(1, mats, feeds, down)
    if packed:
        whole = rest[count + 6]
        places = whole.shape[0] * 2
        widths = (L * 4 * S // places, L * 2 * S // places, L * D // places)
        feed_base = widths[0]
        down_base = feed_base + widths[1] * (SF // S)
        gain_base = down_base + widths[2]
        whole[:, :, gain_base:, :] = jnp.zeros_like(whole[:, :, gain_base:, :])

    def put_at(layer, kind, at, value):
        if not packed:
            target = outs[("attend", "feed", "down", "gain").index(kind)]
            if kind == "gain":
                target[3 * layer + at : 3 * layer + at + 1] = value
            else:
                first = {"attend": (layer * 4 + at) * S, "feed": (layer * 2 + at) * S}.get(
                    kind, layer * D
                )
                target[first : first + value.shape[0]] = value
            return
        if kind == "gain":
            spot = gain_base + 3 * layer + at
            whole[:, :, spot : spot + 1, :] = jnp.broadcast_to(
                value[None, None], whole.shape[:2] + (1, S)
            )
            return
        width = widths[("attend", "feed", "down").index(kind)]
        half = value.shape[0] // width // 2
        if kind == "feed":
            start = (layer * 2 + at) * half
            for column in range(SF // S):
                spot = feed_base + column * width
                whole[start : start + half, :, spot : spot + width, :] = value[
                    :, column * S : (column + 1) * S
                ].reshape(half, 2, width, S)
        else:
            base = 0 if kind == "attend" else down_base
            start = (layer * 4 + at) * half if kind == "attend" else layer * half
            whole[start : start + half, :, base : base + width, :] = value.reshape(
                half, 2, width, S
            )

    work = (flips, grads, grad_flips)
    smalls_one, smalls_two = smalls[0:3], smalls[3:6]
    side_forward(
        tap_two[...],
        down[...],
        state[...],
        mats,
        feeds,
        smalls_two,
        bias,
        saved_two,
        flips,
        result_ref,
    )
    grad_now = side_backward(
        tap_two[...],
        state[...],
        cotangent[...],
        mats,
        feeds,
        smalls_two,
        bias,
        saved_two,
        work,
        partial(put_at, 1),
    )
    load(0, mats, feeds)
    grad_ref[...] = side_backward(
        tap_one[...],
        state_in[...].astype(F32),
        grad_now,
        mats,
        feeds,
        smalls_one,
        bias,
        saved_one,
        work,
        partial(put_at, 0),
    )
    if packed:
        mine = place[0] % 2
        outs[0][...] = whole[:, mine]
        outs[1][...] = whole[:, 1 - mine].astype(BF)


def side_last(places, place, tap_one, tap_two, whole, state_in, state, cotangent, smalls, bias, saved):
    tokens = state.shape[0]
    packed = places > 0
    shapes = [shape_of((tokens, S), F32)] * 2
    scratch = [pltpu.VMEM((tokens, S), kind) for _, kind in SAVED]
    scratch += [
        pltpu.VMEM((2, tokens // ROW, S, ROW), BF),
        pltpu.VMEM((3, tokens, S), F32),
        pltpu.VMEM((tokens // ROW, S, ROW), F32),
    ] + MATRICES
    if packed:
        height = (L * 4 * S + L * 2 * SF + L * D) // places + 16
        shapes += [
            shape_of((places // 2, height, S), F32),
            shape_of((places // 2, height, S), BF),
        ]
        scratch.append(pltpu.VMEM((places // 2, 2, height, S), F32))
    else:
        shapes += [
            shape_of((L * 4 * S, S), F32),
            shape_of((L * 2 * S, SF), F32),
            shape_of((L * D, S), F32),
            shape_of((L * 3, S), F32),
        ]
    return pl.pallas_call(
        partial(side_last_kernel, packed),
        out_shape=shapes,
        in_specs=[SM] + [VM] * (8 + len(SAVED)),
        out_specs=[VM] * len(shapes),
        scratch_shapes=scratch,
        compiler_params=params(32),
        cost_estimate=cost(30.0),
    )(place, tap_one, tap_two, whole, state_in, state, cotangent, smalls, bias, *saved)


def halve_kernel(bit, place, kept, came, keep_ref, send_ref):
    mine = place[2 + bit]
    half = keep_ref.shape[0]
    for at in range(half):
        for target, pick in ((keep_ref, mine), (send_ref, 1 - mine)):
            spot = 2 * at + pick
            target[at] = (kept[spot] + came[spot].astype(F32)).astype(target.dtype)


def halve(bit, place, kept, came):
    half = (kept.shape[0] // 2,) + kept.shape[1:]
    return pl.pallas_call(
        partial(halve_kernel, bit),
        out_shape=[shape_of(half, F32), shape_of(half, BF)],
        in_specs=[SM, VM, VM],
        out_specs=[VM, VM],
        compiler_params=params(16),
    )(place, kept, came)


def tally_kernel(place, kept, came, total_ref, squares_ref):
    total = kept[0] + came[0].astype(F32)
    total_ref[...] = total
    height = total.shape[0]
    squares = total * total
    matrix_part = jnp.sum(squares[: height - 16].reshape(-1, 8, S), axis=0)
    gain_part = jnp.sum(squares[height - 16 :].reshape(-1, 8, S), axis=0)
    squares_ref[...] = matrix_part + jnp.where(place[7] == 0, gain_part, jnp.zeros_like(gain_part))


def tally(place, kept, came):
    return pl.pallas_call(
        tally_kernel,
        out_shape=[shape_of(kept.shape[1:], F32), shape_of((8, S), F32)],
        in_specs=[SM, VM, VM],
        out_specs=[VM, VM],
        compiler_params=params(16),
    )(place, kept, came)


def adamw(master, moment, square, grad_now, clip, rate, decay):
    grad_now = grad_now * clip
    moment = BETA_ONE * moment + (1.0 - BETA_ONE) * grad_now
    square = BETA_TWO * square + (1.0 - BETA_TWO) * grad_now * grad_now
    first_hat = moment / (1.0 - BETA_ONE**STEP)
    second_hat = square / (1.0 - BETA_TWO**STEP)
    master = master - rate * (first_hat / (jnp.sqrt(second_hat) + ADAM_EPS) + decay * master)
    return (master, moment, square)


def update_kernel(total, squares, *refs):
    states, (norm_ref, *outs) = refs[:12], refs[12:]
    grad_norm = jnp.sqrt(jnp.sum(squares[...], keepdims=True))
    norm_ref[...] = grad_norm
    clip = jnp.minimum(1.0, THRESHOLD / grad_norm)
    base = 0
    for at, name in enumerate(("attend", "feed", "down", "gain")):
        master, moment, square = (ref[...] for ref in states[3 * at : 3 * at + 3])
        height, width = master.shape
        columns = []
        for _ in range(width // S):
            columns.append(total[base : base + height])
            base += height
        grad_now = columns[0] if len(columns) == 1 else jnp.concatenate(columns, axis=1)
        rate, decay = (RATE_SMALL, 0.0) if name == "gain" else (RATE_MATRIX, WEIGHT_DECAY)
        new = adamw(master, moment, square, grad_now, clip, rate, decay)
        for value, target in zip(new, outs[:3]):
            target[...] = value
        if name == "gain":
            outs = outs[3:]
        else:
            outs[3][...] = new[0].astype(BF)
            outs = outs[4:]


def update(total, squares, states):
    shapes = [shape_of((1, 1), F32)]
    for at in range(4):
        dims = states[3 * at].shape
        shapes += [shape_of(dims, F32)] * 3
        if at < 3:
            shapes.append(shape_of(dims, BF))
    return pl.pallas_call(
        update_kernel,
        out_shape=shapes,
        in_specs=[VM] * 14,
        out_specs=[VM] * len(shapes),
        compiler_params=params(16),
    )(total, squares, *states)


def swap(value, axis, bit):
    size = lax.axis_size(axis)
    return lax.ppermute(value, axis, [(at, at ^ bit) for at in range(size)])


def join(*values):
    return lax.optimization_barrier(values)


def backbone_rows(
    place,
    frozen_input,
    frozen_attend,
    frozen_output,
    frozen_expand,
    frozen_reduce,
    frozen_gains,
    biases,
    side_own,
    side_layer,
):
    rows = frozen_input.shape[0] // 4
    tokens = rows * ROW
    frozen = (frozen_attend, frozen_output, frozen_expand, frozen_reduce)
    chip_far, chip_own, attend_zero = pack_first(place, frozen_input, *frozen[:2])
    attend_one, feed_zero, feed_one, feed_far = pack(place, *frozen)

    def x(value):
        return swap(value, "head", 2)

    def y(value):
        return swap(value, "batch", 1)

    def z(value):
        return swap(value, "batch", 2)

    def near(value):
        return swap(value, "head", 1)

    def double(value, came):
        return jnp.concatenate([value, came], axis=0)

    wide = shape_of((tokens, D), BF)
    sums = shape_of((tokens, D), F32)

    def attend_own(layer, normed, bias):
        return pl.pallas_call(
            partial(attend_kernel, layer),
            out_shape=shape_of((tokens, BLK), BF),
            in_specs=[VM, HB, VM],
            out_specs=VM,
            scratch_shapes=[
                pltpu.VMEM((3, tokens, BLK), BF),
                pltpu.VMEM((3, D, BLK), BF),
                pltpu.SemaphoreType.DMA((3,)),
            ],
            compiler_params=params(16),
            cost_estimate=cost(3.0),
        )(normed, frozen_attend, bias)

    def attend_far(layer, normed, bias, context, kind, parts):
        return pl.pallas_call(
            partial(attend_far_kernel, layer),
            out_shape=shape_of((tokens, D), kind),
            in_specs=[SM] + [VM] * 3 + [HB] + [VM] * 4,
            out_specs=VM,
            scratch_shapes=[
                pltpu.VMEM((3, tokens, BLK), BF),
                pltpu.VMEM((tokens, BLK), BF),
                pltpu.VMEM((tokens, D), BF),
                pltpu.VMEM((BLK, D), BF),
                pltpu.SemaphoreType.DMA((1,)),
            ],
            compiler_params=params(16),
            cost_estimate=cost(4.0),
        )(place, normed, bias, context, frozen_output, *parts)

    def finish(gain_at, hidden, total, came):
        count = 1 if gain_at is None else 2
        return pl.pallas_call(
            partial(finish_kernel, gain_at),
            out_shape=[wide] * count,
            in_specs=[VM] * 4,
            out_specs=[VM] * count,
            compiler_params=params(12),
            cost_estimate=cost(1.0),
        )(hidden, total, came, frozen_gains)

    def feed_own(layer, normed):
        return pl.pallas_call(
            partial(feed_kernel, layer),
            out_shape=sums,
            in_specs=[VM] + [HB] * 2,
            out_specs=VM,
            scratch_shapes=[
                pltpu.VMEM((2, D, 2 * BLK), BF),
                pltpu.VMEM((2, 2 * BLK, D), BF),
                pltpu.SemaphoreType.DMA((4,)),
            ],
            compiler_params=params(16),
            cost_estimate=cost(3.0),
        )(normed, frozen_expand, frozen_reduce)

    def feed_far_units(normed, totals, parts, kind=F32):
        sets = len(normed)
        return pl.pallas_call(
            partial(feed_far_kernel, len(parts), sets),
            out_shape=[shape_of((tokens, D), kind)] * sets,
            in_specs=[VM] * (2 * sets + len(parts)),
            out_specs=[VM] * sets,
            compiler_params=params(16),
            cost_estimate=cost(1.0 * sets * len(parts)),
        )(*normed, *totals, *parts)

    a0x, near_own = x(attend_zero), near(chip_own)
    side = double(side_own, x(side_own))
    side = double(side, y(side))
    side = double(side, z(side))

    a0x, near_own, chip_far, side = join(a0x, near_own, chip_far, side)
    far, a0y, a0z = x(chip_far), y(a0x), z(a0x)
    side_came = swap(side, "batch", 4)

    far, a0y, a0z, feed_zero, side, side_came = join(far, a0y, a0z, feed_zero, side, side_came)
    far_near, f0x, a0w = near(far), x(feed_zero), y(a0z)
    side = double(side, side_came)
    hidden, normed, other = pl.pallas_call(
        assemble_kernel,
        out_shape=[wide] * 3,
        in_specs=[SM] + [VM] * 5,
        out_specs=[VM] * 3,
        compiler_params=params(16),
        cost_estimate=cost(2.0),
    )(place, chip_own, near_own, far, far_near, frozen_gains)
    context = attend_own(0, normed, biases[0])
    other_context = attend_own(0, other, biases[1])

    context, other_context, a0w, side = join(context, other_context, a0w, side)
    side = double(side, near(side))
    parts = (a0x, a0y, a0z, a0w)
    came = near(attend_far(0, other, biases[1], other_context, BF, parts))
    total = attend_far(0, normed, biases[0], context, F32, parts)
    mid, normed = finish((0, 1), hidden, total, came)

    mid, normed, f0x, attend_one, side = join(mid, normed, f0x, attend_one, side)
    other, a1x, f0y, f0z = near(normed), x(attend_one), y(f0x), z(f0x)
    total = feed_own(0, normed)
    other_total = feed_own(0, other)

    total, other_total, a1x, feed_one = join(total, other_total, a1x, feed_one)
    f1x = x(feed_one)
    f0y, f0z, a1x = join(f0y, f0z, a1x)
    f0w, a1y = z(f0y), y(a1x)
    total, other_total = feed_far_units((normed, other), (total, other_total), (f0x, f0y, f0z))

    total, other_total, f1x, feed_far = join(total, other_total, f1x, feed_far)
    f1w = x(feed_far)
    f0w, a1y, f1x, a1x = join(f0w, a1y, f1x, a1x)
    f1y, a1z = y(f1x), z(a1x)
    came = near(feed_far_units((other,), (other_total,), (f0w,), BF)[0])
    total = feed_far_units((normed,), (total,), (f0w,))[0]
    hidden, normed = finish((1, 0), mid, total, came)
    taps = [hidden]
    other = near(normed)
    context = attend_own(1, normed, biases[0])
    other_context = attend_own(1, other, biases[1])

    context, other_context, a1z, f1x = join(context, other_context, a1z, f1x)
    a1w, f1z = y(a1z), z(f1x)
    side_outs = side_layer(hidden, side)
    a1w, *side_outs = join(a1w, *side_outs)
    parts = (a1x, a1y, a1z, a1w)
    came = near(attend_far(1, other, biases[1], other_context, BF, parts))
    total = attend_far(1, normed, biases[0], context, F32, parts)
    mid, normed = finish((1, 1), hidden, total, came)
    other = near(normed)
    total = feed_own(1, normed)
    other_total = feed_own(1, other)
    total, other_total = feed_far_units((normed, other), (total, other_total), (f1x, f1y))
    total, other_total, f1w, f1z = join(total, other_total, f1w, f1z)
    came = near(feed_far_units((other,), (other_total,), (f1w, f1z), BF)[0])
    total = feed_far_units((normed,), (total,), (f1w, f1z))[0]
    taps.append(finish(None, mid, total, came)[0])
    return (taps, side, side_outs)


def split_attend(normed, w_attend, w_output, same_seg):
    col_count = w_attend.shape[2]
    projected = jnp.einsum(
        "rtd,jdc->jrtc", normed, w_attend, preferred_element_type=jnp.float32
    ).astype(jnp.bfloat16)
    head_shape = normed.shape[:2] + (col_count // HEAD_DIM, HEAD_DIM)
    queries = projected[0].reshape(head_shape)
    key_rows = projected[1].reshape(head_shape)
    value_rows = projected[2].reshape(head_shape)
    scores = jnp.einsum(
        "rqhc,rkhc->rhqk", queries, key_rows, preferred_element_type=jnp.float32
    ) * HEAD_DIM ** (-0.5)
    scores = jnp.where(same_seg[:, None], scores, MASKED)
    shares = jax.nn.softmax(scores, axis=-1).astype(jnp.bfloat16)
    context = jnp.einsum("rhqk,rkhc->rqhc", shares, value_rows, preferred_element_type=jnp.float32)
    context = context.astype(jnp.bfloat16).reshape(normed.shape[:2] + (col_count,))
    return jnp.einsum("rtc,cd->rtd", context, w_output, preferred_element_type=jnp.float32)


def split_feed(normed, w_expand, w_reduce):
    inner = jax.nn.gelu(
        jnp.einsum("rtd,df->rtf", normed, w_expand, preferred_element_type=jnp.float32)
    ).astype(jnp.bfloat16)
    return jnp.einsum("rtf,fd->rtd", inner, w_reduce, preferred_element_type=jnp.float32)


def split_sublayer(hidden, gains, work):
    whole = lax.all_gather(hidden, "head", axis=2, tiled=True)
    normed = root_norm(whole.astype(jnp.float32), gains).astype(jnp.bfloat16)
    summed = lax.psum_scatter(
        work(normed).astype(jnp.bfloat16), "head", scatter_dimension=2, tiled=True
    ).astype(jnp.float32)
    return (hidden.astype(jnp.float32) + summed).astype(jnp.bfloat16)


def backbone_split(
    frozen_input, frozen_attend, frozen_output, frozen_expand, frozen_reduce, frozen_gains, lengths
):
    taps = []
    same_all, _ = segments(lengths)
    hidden = frozen_input
    for layer in range(L):
        hidden = split_sublayer(
            hidden,
            frozen_gains[layer, 0],
            partial(
                split_attend,
                w_attend=frozen_attend[layer],
                w_output=frozen_output[layer],
                same_seg=same_all,
            ),
        )
        hidden = split_sublayer(
            hidden,
            frozen_gains[layer, 1],
            partial(split_feed, w_expand=frozen_expand[layer], w_reduce=frozen_reduce[layer]),
        )
        tapped = lax.all_to_all(hidden, "head", split_axis=0, concat_axis=2, tiled=True)
        taps.append(tapped.reshape(-1, D))
    return taps


def shards(
    frozen_input,
    frozen_attend,
    frozen_output,
    frozen_expand,
    frozen_reduce,
    frozen_gains,
    lengths,
    side_input,
    cotangent,
    attend_master,
    attend_moment,
    attend_square,
    feed_master,
    feed_moment,
    feed_square,
    down_master,
    down_moment,
    down_square,
    gains_master,
    gains_moment,
    gains_square,
):
    head_count, batch_count = lax.axis_size("head"), lax.axis_size("batch")
    tuned = head_count == 4 and batch_count == 8
    head_at, batch_at = lax.axis_index("head"), lax.axis_index("batch")
    own_rows = lengths.shape[0] // head_count
    place = jnp.stack(
        [
            head_at,
            batch_at % 4,
            head_at % 2,
            head_at // 2 % 2,
            batch_at % 2,
            batch_at // 2 % 2,
            batch_at // 4 % 2,
            batch_at * head_count + head_at,
            jnp.zeros_like(head_at),
            gathered_at(batch_at * head_count + head_at) if tuned else jnp.zeros_like(head_at),
        ]
    ).astype(jnp.int32)
    tokens = own_rows * ROW
    state_in = side_input.reshape(tokens, S)
    frozen = (frozen_attend, frozen_output, frozen_expand, frozen_reduce, frozen_gains)
    masters = (attend_master, feed_master, down_master)
    bias, other_bias, grad_seed, *side_own = prepare(
        lengths, place, cotangent.reshape(tokens, S), masters, tuned
    )
    if tuned:
        taps, whole, (*saved, state) = backbone_rows(
            place,
            frozen_input,
            *frozen,
            (bias, other_bias),
            *side_own,
            lambda tap, whole: side_first(place, tap, whole, state_in, gains_master, bias),
        )
    else:
        mats, feeds, downs = (
            lax.all_gather(array.astype(BF), ("batch", "head"), axis=0, tiled=True)
            for array in masters
        )
        feeds = feeds.reshape(PLACES, -1, SF // S, S).transpose(0, 2, 1, 3)
        whole = jnp.concatenate(
            [array.reshape(PLACES, -1, S) for array in (mats, feeds, downs)], axis=1
        )
        whole = whole.reshape((2,) * 5 + whole.shape[1:]).transpose(4, 0, 1, 2, 3, 5, 6)
        whole = whole.reshape(PLACES, -1, S)
        taps = backbone_split(frozen_input, *frozen, lengths)
        *saved, state = side_first(place, taps[0], whole, state_in, gains_master, bias)
    result, input_grad, *sums = side_last(
        PLACES if tuned else 0,
        place,
        *taps,
        whole,
        state_in,
        state,
        grad_seed,
        gains_master,
        bias,
        saved,
    )
    result = result.reshape(cotangent.shape)
    input_grad = input_grad.reshape(cotangent.shape)
    states = (
        attend_master,
        attend_moment,
        attend_square,
        feed_master,
        feed_moment,
        feed_square,
        down_master,
        down_moment,
        down_square,
        gains_master,
        gains_moment,
        gains_square,
    )
    if tuned:
        kept, sent = sums
        came = swap(sent, "head", 1)
        kept, sent = halve(1, place, kept, came)
        came = swap(sent, "head", 2)
        kept, sent = halve(2, place, kept, came)
        came = swap(sent, "batch", 1)
        kept, sent = halve(3, place, kept, came)
        came = swap(sent, "batch", 2)
        kept, sent = halve(4, place, kept, came)
        came = swap(sent, "batch", 4)
        total, squares = tally(place, kept, came)
        for axis, bit in (("head", 1), ("head", 2), ("batch", 1), ("batch", 2), ("batch", 4)):
            squares = squares + swap(squares, axis, bit)
        grad_norm, *rest = update(total, squares, states)
        return (result, input_grad, grad_norm.reshape(()), *rest)
    grads = lax.psum(tuple(sums), ("batch", "head"))
    grad_norm = jnp.sqrt(sum(jnp.sum(grad * grad) for grad in grads))
    clip = jnp.minimum(1.0, THRESHOLD / grad_norm)
    member = lax.axis_index(("batch", "head"))
    outs = []
    for at, grad in enumerate(grads):
        owned = states[3 * at : 3 * at + 3]
        if at < 3:
            height = owned[0].shape[0]
            grad = lax.dynamic_slice_in_dim(grad, member * height, height, 0)
        rate, decay = (RATE_MATRIX, WEIGHT_DECAY) if at < 3 else (RATE_SMALL, 0.0)
        new = adamw(*owned, grad, clip, rate, decay)
        outs.extend(new)
        if at < 3:
            outs.append(new[0].astype(BF))
    return (result, input_grad, grad_norm, *outs)


def solution(mesh):
    row_split = P(("batch", "head"), None)
    cube_split = P(("batch", "head"), None, None)
    return jax.shard_map(
        shards,
        mesh=mesh,
        in_specs=(
            P("batch", None, "head"),
            P(None, None, None, "head"),
            P(None, "head", None),
            P(None, None, "head"),
            P(None, "head", None),
            P(),
            P("batch", None),
            cube_split,
            cube_split,
        )
        + (row_split,) * 9
        + (P(),) * 3,
        out_specs=(cube_split, cube_split, P()) + (row_split,) * 12 + (P(),) * 3,
        check_vma=False,
    )
```

```python
from functools import partial

import jax
import jax.numpy as jnp
from jax import lax
from jax.experimental import pallas as pl
from jax.experimental.pallas import tpu as pltpu
from jax.sharding import PartitionSpec as P

D = 1024
HEAD_DIM = 64
S = 128
SIDE_HD = 8
SF = 512
L = 2
ROW = 128
STEP = 10


NORM_EPS = 1e-06
THRESHOLD = 1.0
BETA_ONE = 0.9
BETA_TWO = 0.999
ADAM_EPS = 1e-08
RATE_MATRIX = 0.12
RATE_SMALL = 0.5
WEIGHT_DECAY = 0.01
MASKED = -1e30

BF = jnp.bfloat16
F32 = jnp.float32
BLK = 256
PLACES = 32
MIB = 2**20

VM = pl.BlockSpec(memory_space=pltpu.VMEM)
SM = pl.BlockSpec(memory_space=pltpu.SMEM)
HB = pl.BlockSpec(memory_space=pltpu.HBM)


def shape_of(dims, kind):
    return jax.ShapeDtypeStruct(dims, kind)


def params(mib):
    return pltpu.CompilerParams(vmem_limit_bytes=mib * MIB)


def cost(micros):
    return pl.CostEstimate(flops=int(micros * 1e6), bytes_accessed=0, transcendentals=0)


def gelu(values):
    squared = values * values
    half = 0.5 * values
    bent = jnp.tanh(values * (0.7978845608028654 + 0.7978845608028654 * 0.044715 * squared))
    return half + half * bent


class Fetch:
    def __init__(self, sems):
        self.sems, self.items = sems, []

    def start(self, source, target):
        item = pltpu.make_async_copy(source, target, self.sems.at[len(self.items)])
        self.items.append(item)
        item.start()
        return item


def nn(a, b):
    return lax.dot_general(a, b, (((1,), (0,)), ((), ())), preferred_element_type=F32)


def nt(a, b):
    return lax.dot_general(a, b, (((1,), (1,)), ((), ())), preferred_element_type=F32)


def norm_scale(values):
    return lax.rsqrt(jnp.mean(values * values, axis=-1, keepdims=True) + NORM_EPS)


def root_norm(values, gains):
    return values * norm_scale(values) * gains


def segments(lengths):
    sent_ends = jnp.cumsum(lengths, axis=-1)
    kept_flag = sent_ends <= ROW
    places = jnp.arange(ROW, dtype=jnp.int32)
    labels = jnp.sum(
        (kept_flag[:, None, :] & (sent_ends[:, None, :] <= places[None, :, None])).astype(
            jnp.int32
        ),
        axis=-1,
    )
    filled = jnp.sum(jnp.where(kept_flag, lengths, 0), axis=-1)
    real_tok = (places[None, :] < filled[:, None]).astype(jnp.float32)
    return (labels[:, :, None] == labels[:, None, :], real_tok)


def side_by_side(rows2):
    return jnp.concatenate([rows2[:ROW], rows2[ROW:]], axis=1)


def block_diagonal(rows2):
    blank = jnp.zeros((ROW, ROW), rows2.dtype)
    top = jnp.concatenate([rows2[:ROW], blank], axis=1)
    low = jnp.concatenate([blank, rows2[ROW:]], axis=1)
    return jnp.concatenate([top, low], axis=0)


def head_masks(head_dim, first):
    lanes = lax.broadcasted_iota(jnp.int32, (ROW, 2 * ROW), 1) % ROW // head_dim
    return (lanes == first, lanes == first + 1)


def stack_heads(wide, masks):
    blank = jnp.zeros_like(wide)
    return jnp.concatenate(
        [jnp.where(masks[0], wide, blank), jnp.where(masks[1], wide, blank)], axis=0
    )


def shares_of(scores, bias, scale):
    scores = scores.reshape(2, ROW, 2 * ROW) + bias[None]
    highest = jnp.max(scores, axis=1, keepdims=True)
    weights = jnp.exp2((scores - highest) * (scale * 1.4426950408889634))
    return weights * (1.0 / jnp.sum(weights, axis=1, keepdims=True))


def head_rows(flipped, count):
    rows = lax.broadcasted_iota(jnp.int32, flipped.shape, 0)
    blank = jnp.zeros_like(flipped)
    return jnp.concatenate(
        [jnp.where(rows < count, flipped, blank), jnp.where(rows >= count, flipped, blank)], axis=1
    )


def diagonal_of(flipped, pair):
    return block_diagonal(jnp.concatenate([flipped[2 * pair], flipped[2 * pair + 1]], axis=0))


def flip(values):
    return values.astype(F32).T


def backbone_heads(proj, bias_ref, context_ref):
    masks = head_masks(HEAD_DIM, 0)
    spots = [
        (pair, slice(pair * 2 * ROW, (pair + 1) * 2 * ROW), slice(lane * ROW, (lane + 1) * ROW))
        for pair in range(proj.shape[1] // (2 * ROW))
        for lane in range(proj.shape[2] // ROW)
    ]
    scores = []
    for _, rows, lanes in spots:
        queries = proj[0, rows, lanes]
        flipped = jnp.concatenate(
            [flip(queries[at * ROW : (at + 1) * ROW]).astype(BF) for at in range(2)], axis=0
        )
        keys = stack_heads(side_by_side(proj[1, rows, lanes]), masks)
        scores.append(nn(keys, block_diagonal(flipped)))
    shares = [
        shares_of(score, bias_ref[pair], HEAD_DIM**-0.5).astype(BF).reshape(2 * ROW, 2 * ROW)
        for score, (pair, _, _) in zip(scores, spots)
    ]
    outs = []
    for share, (_, rows, lanes) in zip(shares, spots):
        values = proj[2, rows, lanes]
        for at in range(2):
            flipped = flip(values[at * ROW : (at + 1) * ROW]).astype(BF)
            out = nn(head_rows(flipped, HEAD_DIM), share[:, at * ROW : (at + 1) * ROW])
            outs.append(out.T.astype(BF))
    for index, (_, rows, lanes) in enumerate(spots):
        for at in range(2):
            start = rows.start + at * ROW
            context_ref[start : start + ROW, lanes] = outs[2 * index + at]


def assemble_kernel(place, own, near, far, far_near, gains, hidden_ref, normed_ref):
    rows = own.shape[0] // 2
    mine = pl.ds(place[2] * rows, rows)
    for step, piece in enumerate((own, near, far, far_near)):
        spot = pl.multiple_of((place[0] ^ step) * BLK, BLK)
        hidden_ref[:, pl.ds(spot, BLK)] = piece[mine].reshape(rows * ROW, BLK)
    normed_ref[...] = root_norm(hidden_ref[...].astype(F32), gains[0, 0:1]).astype(BF)


def split_rows(total, count):
    heights = [(total // count + 15) // 16 * 16] * (count - 1)
    return heights + [total - sum(heights)]


def load_rows(refs):
    return refs[0][...] if len(refs) == 1 else jnp.concatenate([ref[...] for ref in refs], axis=0)


def store_rows(refs, columns, value):
    start = 0
    for ref in refs:
        ref[:, columns] = value[start : start + ref.shape[0]].astype(ref.dtype)
        start += ref.shape[0]


def attend_kernel(layer, normed, weights, bias, context, proj, held, sems):
    fetch = Fetch(sems)
    waits = [fetch.start(weights.at[layer, at], held.at[at]) for at in range(3)]
    for at in range(3):
        waits[at].wait()
        proj[at] = nn(normed[...], held[at]).astype(BF)
    backbone_heads(proj, bias, context)


def attend_far_kernel(
    layer, place, normed, bias, hidden, gains, context_a, context_b, out_a, out_b, *rest
):
    parts, (mid_ref, normed_ref, *sent) = rest[:8], rest[8:-6]
    proj, context, total, turned, held, sems = rest[-6:]
    fetch = Fetch(sems)
    waits = [
        fetch.start(source.at[layer], held.at[pl.ds(at * BLK, BLK)])
        for at, source in enumerate((out_a, out_b))
    ]
    spots = [pl.ds(pl.multiple_of((place[1] ^ step) * BLK, BLK), BLK) for step in range(4)]
    for step, spot in enumerate(spots):
        turned[:, step * BLK : (step + 1) * BLK] = normed[:, spot]
    for slot, group in enumerate((parts[:4], parts[4:])):
        for at in range(3):
            weights = jnp.concatenate([part[at] for part in group], axis=0)
            proj[slot, at] = nn(turned[...], weights).astype(BF)
        backbone_heads(proj.at[slot], bias, context.at[slot])
    for item in waits:
        item.wait()
    both = jnp.concatenate([context_a[...], context_b[...], context[0], context[1]], axis=1)
    for step, spot in enumerate(spots):
        weights = jnp.concatenate([held[:, spot], parts[step][3], parts[4 + step][3]], axis=0)
        total[:, spot] = hidden[:, spot].astype(F32) + nn(both, weights)
    mid = total[...].astype(BF)
    mid_ref[...] = mid
    normed_now = root_norm(mid.astype(F32), gains[layer, 1:2])
    store_rows((normed_ref,), slice(None), normed_now)
    store_rows(sent, slice(None), normed_now)


def finish_kernel(gain_at, count, hidden, total, gains, *refs):
    outs = refs[count:]
    came = load_rows(refs[:count]).astype(F32)
    value = (hidden[...].astype(F32) + (total[...] + came)).astype(BF)
    outs[0][...] = value
    if gain_at is not None:
        layer, at = gain_at
        outs[1][...] = root_norm(value.astype(F32), gains[layer, at : at + 1]).astype(BF)


def feed_kernel(layer, count, *refs):
    normed, (expand, reduce, total_ref) = refs[:count], refs[count:]
    values = load_rows(normed)
    for at in range(expand.shape[2] // (2 * BLK)):
        units = slice(at * 2 * BLK, (at + 1) * 2 * BLK)
        inner = gelu(nn(values, expand[layer, :, units])).astype(BF)
        term = nn(inner, reduce[layer, units, :])
        if at == 0:
            total_ref[...] = term
        else:
            total_ref[...] += term


def feed_far_kernel(counts, layout, *refs):
    refs = list(refs)

    def take(count):
        taken = refs[:count]
        del refs[:count]
        return taken

    sets = [take(count) for count in counts]
    totals = take(len(counts))
    outs = [refs[len(refs) - sum(layout) :][sum(layout[:at]) : sum(layout[: at + 1])] for at in range(len(counts))]
    parts = refs[: len(refs) - sum(layout)]
    for normed, total, out in zip(sets, totals, outs):
        values = load_rows(normed)
        inners = [gelu(nn(values, part[0:4].reshape(D, BLK))).astype(BF) for part in parts]
        inner = jnp.concatenate(inners, axis=1)
        for at in range(4):
            weights = jnp.concatenate([part[4 + at] for part in parts], axis=0)
            columns = slice(at * BLK, (at + 1) * BLK)
            store_rows(out, columns, total[:, columns] + nn(inner, weights))


def pack_first_kernel(place, attend, output, attend_part, sems):
    fetch = Fetch(sems)
    spot = pl.ds(pl.multiple_of(place[1] * BLK, BLK), BLK)
    for at in range(3):
        fetch.start(attend.at[0, at, spot, :], attend_part.at[at])
    fetch.start(output.at[0, :, spot], attend_part.at[3])
    for item in fetch.items:
        item.wait()


def pack_first(place, attend, output):
    return pl.pallas_call(
        pack_first_kernel,
        out_shape=shape_of((4, BLK, BLK), BF),
        in_specs=[SM] + [HB] * 2,
        out_specs=VM,
        scratch_shapes=[pltpu.SemaphoreType.DMA((4,))],
        compiler_params=params(57),
        cost_estimate=cost(1.0),
    )(place, attend, output)


def split_chip_kernel(place, hidden, chip_far, chip_own, sems):
    fetch = Fetch(sems)
    rows = chip_own.shape[0]
    fetch.start(hidden.at[pl.ds((1 - place[3]) * rows, rows)], chip_far)
    fetch.start(hidden.at[pl.ds(place[3] * rows, rows)], chip_own)
    for item in fetch.items:
        item.wait()


def split_chip(place, hidden):
    half = (hidden.shape[0] // 2,) + hidden.shape[1:]
    return pl.pallas_call(
        split_chip_kernel,
        out_shape=[shape_of(half, BF)] * 2,
        in_specs=[SM, HB],
        out_specs=[VM] * 2,
        scratch_shapes=[pltpu.SemaphoreType.DMA((2,))],
        compiler_params=params(4),
        cost_estimate=cost(1.0),
    )(place, hidden)


def pack_kernel(place, attend, output, expand, reduce, attend_part, attend_other, *rest):
    feed_targets, sems = rest[:-1], rest[-1]
    fetch = Fetch(sems)
    spot = pl.ds(pl.multiple_of(place[1] * BLK, BLK), BLK)
    last = pl.ds(pl.multiple_of((place[1] ^ 3) * BLK, BLK), BLK)
    for layer, units, target in zip((0, 1, 1), (spot, spot, last), feed_targets):
        for at in range(4):
            rows = pl.ds(at * BLK, BLK)
            fetch.start(expand.at[layer, rows, units], target.at[at])
            fetch.start(reduce.at[layer, units, rows], target.at[4 + at])
    other = pl.ds(pl.multiple_of((place[1] ^ 2) * BLK, BLK), BLK)
    for rows, target in ((spot, attend_part), (other, attend_other)):
        for at in range(3):
            fetch.start(attend.at[1, at, rows, :], target.at[at])
        fetch.start(output.at[1, :, rows], target.at[3])
    for item in fetch.items:
        item.wait()


def pack(place, attend, output, expand, reduce):
    return pl.pallas_call(
        pack_kernel,
        out_shape=[shape_of((4, BLK, BLK), BF)] * 2 + [shape_of((8, BLK, BLK), BF)] * 3,
        in_specs=[SM] + [HB] * 4,
        out_specs=[VM] * 5,
        scratch_shapes=[pltpu.SemaphoreType.DMA((32,))],
        compiler_params=params(57),
        cost_estimate=cost(2.0),
    )(place, attend, output, expand, reduce)


def prepare_kernel(lengths, place, cotangent, *rest):
    masters, (bias_ref, seed_ref, *packed) = rest[:3], rest[3:]
    rows = cotangent.shape[0] // ROW
    deep = lax.broadcasted_iota(jnp.int32, (ROW, ROW), 0)
    across = lax.broadcasted_iota(jnp.int32, (ROW, ROW), 1)
    for row in range(rows):
        end = jnp.int32(0)
        filled = jnp.int32(0)
        deep_label = jnp.zeros((ROW, ROW), jnp.int32)
        across_label = jnp.zeros((ROW, ROW), jnp.int32)
        for slot in range(lengths.shape[0]):
            length = lengths[slot, place[0] * rows + row]
            end = end + length
            kept = end <= ROW
            filled = filled + jnp.where(kept, length, 0)
            start = jnp.where(kept, end, ROW)
            deep_label += (deep >= start).astype(jnp.int32)
            across_label += (across >= start).astype(jnp.int32)
        pair, at = row // 2, row % 2
        bias_ref[pair, :, at * ROW : (at + 1) * ROW] = jnp.where(
            deep_label == across_label, 0.0, MASKED
        )
        spot = slice(row * ROW, (row + 1) * ROW)
        seed_ref[spot] = jnp.where(deep < filled, cotangent[spot], 0.0)
    if packed:
        base = 0
        for master in masters:
            height, width = master.shape
            for column in range(width // S):
                packed[0][0, base : base + height] = master[:, column * S : (column + 1) * S].astype(BF)
                base += height


def prepare(lengths, place, cotangent, masters, packed):
    tokens = cotangent.shape[0]
    shapes = [shape_of((tokens // ROW // 2, ROW, 2 * ROW), F32), shape_of((tokens, S), F32)]
    if packed:
        shapes.append(shape_of((1, sum(master.size for master in masters) // S, S), BF))
    return pl.pallas_call(
        prepare_kernel,
        out_shape=shapes,
        in_specs=[SM, SM] + [VM] * 4,
        out_specs=[VM] * len(shapes),
        compiler_params=params(57),
        cost_estimate=cost(1.5),
    )(lengths.T, place, cotangent, *masters)


TURNS = S // SIDE_HD // 2
GROUP = 8


def head_spot(turn):
    return pl.ds(pl.multiple_of(turn * 2 * SIDE_HD, 2 * SIDE_HD), 2 * SIDE_HD)


def saved_shapes(tokens):
    return {
        "tapped": ((tokens, S), F32),
        "mixed": ((tokens, S), F32),
        "middle": ((tokens, S), F32),
        "queries": ((tokens, S), BF),
        "keys": ((tokens, S), BF),
        "values": ((tokens, S), BF),
        "context": ((tokens // ROW, S, ROW), F32),
        "shares": ((tokens // (2 * ROW) * TURNS, 2 * ROW, 2 * ROW), BF),
    }


def flip_rows(source, target):
    for at in range(target.shape[0]):
        target[at] = flip(source[at * ROW : (at + 1) * ROW]).astype(target.dtype)


def rows_side_by_side(source):
    return jnp.concatenate([source[at] for at in range(source.shape[0])], axis=1)


def query_rows(flipped, first, spot):
    top, low = flipped[first, spot], flipped[first + 1, spot]
    blank = jnp.zeros_like(top)
    return jnp.concatenate(
        [jnp.concatenate([top, blank], axis=1), jnp.concatenate([blank, low], axis=1)], axis=0
    )


def key_rows(flipped, first, spot):
    return jnp.concatenate(
        [head_rows(flipped[first + at, spot], SIDE_HD) for at in range(2)], axis=0
    )


def gathered_at(device):
    order = (4, 3, 2, 1, 0)
    return sum((device >> bit & 1) << at for at, bit in enumerate(order))


def matrix_loader(place, whole, places):
    heights = (L * 4 * S // places, L * 2 * S // places, L * D // places)
    feed_base = heights[0]
    down_base = feed_base + heights[1] * (SF // S)

    def rows(first, total, base, height):
        start = first // height
        return jnp.concatenate(
            [
                whole[gathered_at(start + step) ^ place[9], base : base + height]
                for step in range(total // height)
            ],
            axis=0,
        )

    def load(layer, mats, feeds, down=None):
        for at in range(4):
            mats[at] = rows((layer * 4 + at) * S, S, 0, heights[0])
        for at in range(2):
            for column in range(SF // S):
                feeds[at, :, column * S : (column + 1) * S] = rows(
                    (layer * 2 + at) * S, S, feed_base + column * heights[1], heights[1]
                )
        if down is not None:
            down[...] = rows(layer * D, D, down_base, heights[2])

    return load


def side_forward(tap_source, down, state, mats, feeds, smalls, bias_ref, saved, flips, result_ref):
    tokens = state.shape[0]
    gating = jax.nn.sigmoid(smalls[2:3])
    tapped = nn(tap_source, down)
    mixed = gating * tapped + (1.0 - gating) * state
    saved["tapped"][...] = tapped
    saved["mixed"][...] = mixed
    normed = (mixed * norm_scale(mixed) * smalls[0:1]).astype(BF)
    for at, name in enumerate(("queries", "keys", "values")):
        saved[name][...] = nn(normed, mats[at]).astype(BF)
    flip_rows(saved["values"], flips.at[0])
    flip_rows(saved["queries"], flips.at[1])
    groups = TURNS // GROUP

    def step(index, carry):
        pair, first = index // groups, index % groups * GROUP
        rows = pl.ds(pl.multiple_of(pair * 2 * ROW, 2 * ROW), 2 * ROW)
        keys = side_by_side(saved["keys"][rows])
        stacks = [stack_heads(keys, head_masks(SIDE_HD, 2 * (first + at))) for at in range(GROUP)]
        scores = nn(jnp.concatenate(stacks, axis=0), diagonal_of(flips.at[1], pair))
        bias = bias_ref[pair]
        spots = [head_spot(first + at) for at in range(GROUP)]
        lefts = [key_rows(flips.at[0], 2 * pair, spot) for spot in spots]
        shares, outs = [], []
        for at in range(GROUP):
            own = shares_of(scores[at * 2 * ROW : (at + 1) * 2 * ROW], bias, SIDE_HD**-0.5)
            shares.append(own.astype(BF).reshape(2 * ROW, 2 * ROW))
            outs.append(nn(lefts[at], shares[-1]))
        for at, spot in enumerate(spots):
            saved["shares"][pair * TURNS + first + at] = shares[at]
            saved["context"][2 * pair, spot] = outs[at][: 2 * SIDE_HD, :ROW]
            saved["context"][2 * pair + 1, spot] = outs[at][2 * SIDE_HD :, ROW:]
        return carry

    lax.fori_loop(0, tokens // (2 * ROW) * groups, step, 0)
    context = jnp.concatenate(
        [saved["context"][at].T.astype(BF) for at in range(tokens // ROW)], axis=0
    )
    middle = mixed + nn(context, mats[3])
    saved["middle"][...] = middle
    normed_two = (middle * norm_scale(middle) * smalls[1:2]).astype(BF)
    active = gelu(nn(normed_two, feeds[0])).astype(BF)
    result_ref[...] = middle + nt(active, feeds[1])


def gelu_parts(inner):
    root = 0.7978845608028654
    squared = inner * inner
    bent = jnp.tanh(root * inner * (1.0 + 0.044715 * squared))
    half = 0.5 * (1.0 + bent)
    slope = half + 0.5 * inner * (1.0 - bent * bent) * (root * (1.0 + 3.0 * 0.044715 * squared))
    return (inner * half, slope)


def norm_back(values, scale, gains, grad_normed):
    weighted = grad_normed * gains
    grad_values = scale * weighted - values * scale**3 * jnp.mean(
        weighted * values, axis=-1, keepdims=True
    )
    return (grad_values, jnp.sum(grad_normed * values * scale, axis=0, keepdims=True))


def side_backward(tap_source, state, grad_out, mats, feeds, smalls, bias_ref, saved, work, put):
    flips, grad_flips, means = work
    tokens = grad_out.shape[0]
    pairs = tokens // (2 * ROW)
    middle = saved["middle"][...]
    second_scale = norm_scale(middle)
    normed_two = (middle * second_scale * smalls[1:2]).astype(BF)
    active, slope = gelu_parts(nn(normed_two, feeds[0]))
    grad_outer = grad_out.astype(BF)
    put("feed", 1, nn(flip(grad_outer).astype(BF), active.astype(BF)))
    grad_inner = (nn(grad_outer, feeds[1]) * slope).astype(BF)
    put("feed", 0, nn(flip(normed_two).astype(BF), grad_inner))
    grad_middle, grad_gain_two = norm_back(
        middle, second_scale, smalls[1:2], nt(grad_inner, feeds[0])
    )
    put("gain", 1, grad_gain_two)
    grad_middle = grad_middle + grad_out
    grad_branch = grad_middle.astype(BF)
    context_flip = rows_side_by_side(saved["context"])
    put("attend", 3, nn(context_flip.astype(BF), grad_branch))
    grad_context = nt(mats[3], grad_branch).astype(BF)
    for at in range(tokens // ROW):
        flips[2, at] = grad_context[:, at * ROW : (at + 1) * ROW]
    flip_rows(saved["queries"], flips.at[0])
    flip_rows(saved["keys"], flips.at[1])
    products = (grad_context.astype(F32) * context_flip).reshape(S // SIDE_HD, SIDE_HD, tokens)
    sums = jnp.sum(products, axis=1)
    for pair in range(pairs):
        for head in range(TURNS):
            means[pair * TURNS + head] = sums[
                2 * head : 2 * head + 2, pair * 2 * ROW : (pair + 1) * 2 * ROW
            ]

    groups = TURNS // GROUP

    def step(index, carry):
        pair, first = index // groups, index % groups * GROUP
        rows = pl.ds(pl.multiple_of(pair * 2 * ROW, 2 * ROW), 2 * ROW)
        values = side_by_side(saved["values"][rows])
        stacks = [stack_heads(values, head_masks(SIDE_HD, 2 * (first + at))) for at in range(GROUP)]
        products = nn(jnp.concatenate(stacks, axis=0), diagonal_of(flips.at[2], pair))
        turns = [pair * TURNS + first + at for at in range(GROUP)]
        spots = [head_spot(first + at) for at in range(GROUP)]
        shares = [saved["shares"][turn] for turn in turns]
        centres = [means[turn].reshape(2, 1, 2 * ROW) for turn in turns]
        key_lefts = [key_rows(flips.at[1], 2 * pair, spot) for spot in spots]
        query_lefts = [query_rows(flips.at[0], 2 * pair, spot) for spot in spots]
        grad_lefts = [query_rows(flips.at[2], 2 * pair, spot) for spot in spots]
        upper = lax.broadcasted_iota(jnp.int32, (2 * SIDE_HD, ROW), 0) < SIDE_HD
        outs = []
        for at in range(GROUP):
            grad = products[at * 2 * ROW : (at + 1) * 2 * ROW].reshape(2, ROW, 2 * ROW)
            grad = shares[at].astype(F32).reshape(2, ROW, 2 * ROW) * (grad - centres[at])
            grad = grad.astype(BF).reshape(2 * ROW, 2 * ROW)
            outs.append(
                (
                    nn(key_lefts[at], grad),
                    nt(query_lefts[at], grad),
                    nt(grad_lefts[at], shares[at]),
                )
            )
        for spot, (query_part, *others) in zip(spots, outs):
            grad_flips[0, 2 * pair, spot] = query_part[: 2 * SIDE_HD, :ROW]
            grad_flips[0, 2 * pair + 1, spot] = query_part[2 * SIDE_HD :, ROW:]
            for slot, out in enumerate(others):
                for at in range(2):
                    half = out[at * 2 * SIDE_HD : (at + 1) * 2 * SIDE_HD]
                    grad_flips[1 + slot, 2 * pair + at, spot] = jnp.where(
                        upper, half[:, :ROW], half[:, ROW:]
                    )
        return carry

    lax.fori_loop(0, pairs * groups, step, 0)
    root = SIDE_HD**-0.5
    mixed = saved["mixed"][...]
    first_scale = norm_scale(mixed)
    normed_flip = flip((mixed * first_scale * smalls[0:1]).astype(BF)).astype(BF)
    grad_normed = None
    for at, factor in enumerate((root, root, None)):
        grad = rows_side_by_side(grad_flips.at[at])
        grad = (grad if factor is None else grad * factor).astype(BF)
        put("attend", at, nt(normed_flip, grad))
        term = nn(mats[at], grad)
        grad_normed = term if grad_normed is None else grad_normed + term
    grad_normed = grad_normed.T
    grad_mixed, grad_gain_one = norm_back(mixed, first_scale, smalls[0:1], grad_normed)
    put("gain", 0, grad_gain_one)
    grad_mixed = grad_mixed + grad_middle
    gating = jax.nn.sigmoid(smalls[2:3])
    grad_tap = (gating * grad_mixed).astype(BF)
    put(
        "gain",
        2,
        jnp.sum(grad_mixed * (saved["tapped"][...] - state), axis=0, keepdims=True)
        * gating
        * (1.0 - gating),
    )
    put("down", 0, nn(flip(grad_tap).astype(BF), tap_source).T)
    return (1.0 - gating) * grad_mixed


MATRICES = [
    pltpu.VMEM((4, S, S), BF),
    pltpu.VMEM((2, S, SF), BF),
    pltpu.VMEM((D, S), BF),
]


def side_first_kernel(place, tap_source, whole, state, smalls, bias, *rest):
    outs, (flips, mats, feeds, down) = rest[:-4], rest[-4:]
    matrix_loader(place, whole, PLACES)(0, mats, feeds, down)
    saved = dict(zip(saved_shapes(state.shape[0]), outs))
    side_forward(
        tap_source[...],
        down[...],
        state[...].astype(F32),
        mats,
        feeds,
        smalls[0:3],
        bias,
        saved,
        flips,
        outs[-1],
    )


def side_first(place, tap_source, whole, state, smalls, bias):
    tokens = state.shape[0]
    return pl.pallas_call(
        side_first_kernel,
        out_shape=[shape_of(*item) for item in saved_shapes(tokens).values()]
        + [shape_of((tokens, S), F32)],
        in_specs=[SM] + [VM] * 5,
        out_specs=[VM] * (len(saved_shapes(tokens)) + 1),
        scratch_shapes=[pltpu.VMEM((2, tokens // ROW, S, ROW), BF)] + MATRICES,
        compiler_params=params(16),
        cost_estimate=cost(8.0),
    )(place, tap_source, whole, state, smalls, bias)


def side_last_kernel(
    packed,
    place,
    tap_one,
    tap_two,
    whole_in,
    state_in,
    state,
    cotangent,
    smalls,
    bias,
    *rest,
):
    names = saved_shapes(cotangent.shape[0])
    count = len(names)
    saved_one = dict(zip(names, rest[:count]))
    rest = rest[count:]
    result_ref, grad_ref = rest[:2]
    outs = rest[2:5] if packed else rest[2:6]
    rest = rest[len(outs) + 2 :]
    saved_two = dict(zip(names, rest[:count]))
    work = rest[count : count + 3]
    mats, feeds, down = rest[count + 3 : count + 6]
    load = matrix_loader(place, whole_in, PLACES)
    load(1, mats, feeds, down)
    if packed:
        places = outs[0].shape[0] * 2
        widths = (L * 4 * S // places, L * 2 * S // places, L * D // places)
        feed_base = widths[0]
        down_base = feed_base + widths[1] * (SF // S)
        even = place[2] == 0
        outs[2][...] = jnp.zeros_like(outs[2])

    def put_rows(start, base, value):
        kept = jnp.where(even, value[:, 0], value[:, 1])
        sent = jnp.where(even, value[:, 1], value[:, 0])
        spot = (slice(start, start + value.shape[0]), slice(base, base + value.shape[2]))
        outs[0][spot] = kept
        outs[1][spot] = sent.astype(BF)

    def put_at(layer, kind, at, value):
        if not packed:
            target = outs[("attend", "feed", "down", "gain").index(kind)]
            if kind == "gain":
                target[3 * layer + at : 3 * layer + at + 1] = value
            else:
                first = {"attend": (layer * 4 + at) * S, "feed": (layer * 2 + at) * S}.get(
                    kind, layer * D
                )
                target[first : first + value.shape[0]] = value
            return
        if kind == "gain":
            outs[2][8 + 3 * layer + at : 9 + 3 * layer + at] = value
            return
        width = widths[("attend", "feed", "down").index(kind)]
        half = value.shape[0] // width // 2
        if kind == "feed":
            start = (layer * 2 + at) * half
            for column in range(SF // S):
                part = value[:, column * S : (column + 1) * S].reshape(half, 2, width, S)
                put_rows(start, feed_base + column * width, part)
        else:
            base = 0 if kind == "attend" else down_base
            start = (layer * 4 + at) * half if kind == "attend" else layer * half
            put_rows(start, base, value.reshape(half, 2, width, S))

    smalls_one, smalls_two = smalls[0:3], smalls[3:6]
    side_forward(
        tap_two[...],
        down[...],
        state[...],
        mats,
        feeds,
        smalls_two,
        bias,
        saved_two,
        work[0],
        result_ref,
    )
    grad_now = side_backward(
        tap_two[...],
        state[...],
        cotangent[...],
        mats,
        feeds,
        smalls_two,
        bias,
        saved_two,
        work,
        partial(put_at, 1),
    )
    load(0, mats, feeds)
    grad_ref[...] = side_backward(
        tap_one[...],
        state_in[...].astype(F32),
        grad_now,
        mats,
        feeds,
        smalls_one,
        bias,
        saved_one,
        work,
        partial(put_at, 0),
    )


def side_last(places, place, tap_one, tap_two, whole, state_in, state, cotangent, smalls, bias, saved):
    tokens = state.shape[0]
    packed = places > 0
    shapes = [shape_of((tokens, S), F32)] * 2
    scratch = [pltpu.VMEM(*item) for item in saved_shapes(tokens).values()]
    scratch += [
        pltpu.VMEM((3, tokens // ROW, S, ROW), BF),
        pltpu.VMEM((3, tokens // ROW, S, ROW), F32),
        pltpu.VMEM((tokens // (2 * ROW) * TURNS, 2, 2 * ROW), F32),
    ] + MATRICES
    if packed:
        height = (L * 4 * S + L * 2 * SF + L * D) // places
        shapes += [
            shape_of((places // 2, height, S), F32),
            shape_of((places // 2, height, S), BF),
            shape_of((16, S), F32),
        ]
    else:
        shapes += [
            shape_of((L * 4 * S, S), F32),
            shape_of((L * 2 * S, SF), F32),
            shape_of((L * D, S), F32),
            shape_of((L * 3, S), F32),
        ]
    return pl.pallas_call(
        partial(side_last_kernel, packed),
        out_shape=shapes,
        in_specs=[SM] + [VM] * (8 + len(saved)),
        out_specs=[VM] * len(shapes),
        scratch_shapes=scratch,
        compiler_params=params(32),
        cost_estimate=cost(30.0),
    )(place, tap_one, tap_two, whole, state_in, state, cotangent, smalls, bias, *saved)


ROW_GROUPS = (64, 48, 48)
LINKS = {"x": ("head", 2, 3), "y": ("batch", 1, 4), "z": ("batch", 2, 5), "far z": ("batch", 4, 6)}
TURNS_OF_GROUPS = (("x", "y", "z"), ("y", "z", "x"), ("z", "x", "y"))


def halve_kernel(whole, steps, place, *refs):
    count = len(steps)
    sources = refs[: 2 if whole else 2 * count]
    outs = refs[len(sources) :]
    start = 0
    for group, (slot, position) in enumerate(steps):
        kept, came = sources[:2] if whole else sources[2 * group : 2 * group + 2]
        keep_ref, send_ref = outs[2 * group : 2 * group + 2]
        half, height = keep_ref.shape[:2]
        rows = slice(start, start + height) if whole else slice(None)
        start += height
        mine = place[slot]
        for at in range(half):
            base = (at >> position << position + 1) + at % (1 << position)
            for target, pick in ((keep_ref, mine), (send_ref, 1 - mine)):
                spot = base + (pick << position)
                value = kept[spot, rows] + came[spot, rows].astype(F32)
                target[at] = value.astype(target.dtype)


def halve(place, steps, heights, pairs):
    whole = len(pairs) == 1
    half = pairs[0][0].shape[0] // 2
    shapes = []
    for height in heights:
        shapes += [shape_of((half, height, S), F32), shape_of((half, height, S), BF)]
    flat = [array for pair in pairs for array in pair]
    outs = pl.pallas_call(
        partial(halve_kernel, whole, steps),
        out_shape=shapes,
        in_specs=[SM] + [VM] * len(flat),
        out_specs=[VM] * len(shapes),
        compiler_params=params(16),
        cost_estimate=cost(0.6),
    )(place, *flat)
    return list(zip(outs[::2], outs[1::2]))


def regroup_kernel(*refs):
    sources, (kept_ref, sent_ref) = refs[:-2], refs[-2:]
    start = 0
    for kept, came in zip(sources[::2], sources[1::2]):
        rows = slice(start, start + kept.shape[1])
        start += kept.shape[1]
        value = (kept[...] + came[...].astype(F32)).astype(BF)
        kept_ref[:, rows] = value
        sent_ref[:, rows] = value


def scatter_sums(place, kept, sent):
    def exchange(name, value):
        axis, bit, _ = LINKS[name]
        return swap(value, axis, bit)

    pairs = [(kept, swap(sent, "head", 1))]
    left = [["x", "y", "z", "far z"] for _ in ROW_GROUPS]
    for turn in range(3):
        steps = []
        for group, names in enumerate(left):
            name = TURNS_OF_GROUPS[group][turn]
            steps.append((LINKS[name][2], names.index(name)))
            names.remove(name)
        halves = halve(place, tuple(steps), ROW_GROUPS, pairs)
        pairs = [
            (keep, exchange(TURNS_OF_GROUPS[group][turn], send))
            for group, (keep, send) in enumerate(halves)
        ]
    shape = shape_of((2, sum(ROW_GROUPS), S), BF)
    kept, sent = pl.pallas_call(
        regroup_kernel,
        out_shape=[shape] * 2,
        in_specs=[VM] * 6,
        out_specs=[VM] * 2,
        compiler_params=params(16),
        cost_estimate=cost(0.6),
    )(*(array for pair in pairs for array in pair))
    return (kept, exchange("far z", sent))


def tally_kernel(place, kept, came, small, total_ref, small_ref):
    total = kept[...].astype(F32) + came[...].astype(F32)
    squares = total * total
    total_ref[...] = jnp.where(place[LINKS["far z"][2]] == 0, total[0], total[1])
    small_ref[0:8] = jnp.sum(squares.reshape(-1, 8, S), axis=0)
    small_ref[8:16] = small[8:16]


def tally(place, kept, came, small):
    return pl.pallas_call(
        tally_kernel,
        out_shape=[shape_of(kept.shape[1:], F32), shape_of((16, S), F32)],
        in_specs=[SM] + [VM] * 3,
        out_specs=[VM] * 2,
        compiler_params=params(16),
        cost_estimate=cost(0.6),
    )(place, kept, came, small)


def adamw(master, moment, square, grad_now, clip, rate, decay):
    grad_now = grad_now * clip
    moment = BETA_ONE * moment + (1.0 - BETA_ONE) * grad_now
    square = BETA_TWO * square + (1.0 - BETA_TWO) * grad_now * grad_now
    first_hat = moment / (1.0 - BETA_ONE**STEP)
    second_hat = square / (1.0 - BETA_TWO**STEP)
    master = master - rate * (first_hat / (jnp.sqrt(second_hat) + ADAM_EPS) + decay * master)
    return (master, moment, square)


def update_kernel(total, squares, *refs):
    states, (norm_ref, *outs) = refs[:12], refs[12:]
    gains = squares[8:16]
    grad_norm = jnp.sqrt(jnp.sum(squares[0:8] + gains * gains, keepdims=True))
    norm_ref[...] = grad_norm
    clip = jnp.minimum(1.0, THRESHOLD / grad_norm)
    base = 0
    for at, name in enumerate(("attend", "feed", "down", "gain")):
        master, moment, square = (ref[...] for ref in states[3 * at : 3 * at + 3])
        height, width = master.shape
        columns = []
        for _ in range(width // S):
            source = gains[:height] if name == "gain" else total[base : base + height]
            columns.append(source)
            base += height
        grad_now = columns[0] if len(columns) == 1 else jnp.concatenate(columns, axis=1)
        rate, decay = (RATE_SMALL, 0.0) if name == "gain" else (RATE_MATRIX, WEIGHT_DECAY)
        new = adamw(master, moment, square, grad_now, clip, rate, decay)
        for value, target in zip(new, outs[:3]):
            target[...] = value
        if name == "gain":
            outs = outs[3:]
        else:
            outs[3][...] = new[0].astype(BF)
            outs = outs[4:]


def update(total, squares, states):
    shapes = [shape_of((1, 1), F32)]
    for at in range(4):
        dims = states[3 * at].shape
        shapes += [shape_of(dims, F32)] * 3
        if at < 3:
            shapes.append(shape_of(dims, BF))
    return pl.pallas_call(
        update_kernel,
        out_shape=shapes,
        in_specs=[VM] * 14,
        out_specs=[VM] * len(shapes),
        compiler_params=params(16),
    )(total, squares, *states)


def swap(value, axis, bit):
    size = lax.axis_size(axis)
    return lax.ppermute(value, axis, [(at, at ^ bit) for at in range(size)])


def join(*values):
    return lax.optimization_barrier(values)


def backbone_rows(
    place,
    frozen_input,
    frozen_attend,
    frozen_output,
    frozen_expand,
    frozen_reduce,
    frozen_gains,
    attend_zero,
    bias,
    side_own,
    side_layer,
):
    rows = frozen_input.shape[0] // 4
    tokens = rows * ROW
    frozen = (frozen_attend, frozen_output, frozen_expand, frozen_reduce)
    chip_far, chip_own = split_chip(place, frozen_input)
    attend_one, attend_other, feed_zero, feed_one, feed_other = pack(place, *frozen)

    def x(value):
        return swap(value, "head", 2)

    def y(value):
        return swap(value, "batch", 1)

    def z(value):
        return swap(value, "batch", 2)

    def near(value):
        return swap(value, "head", 1)

    def double(value, came):
        return jnp.concatenate([value, came], axis=0)

    wide = shape_of((tokens, D), BF)
    sums = shape_of((tokens, D), F32)


    def attend_own(layer, normed, weights):
        return pl.pallas_call(
            partial(attend_kernel, layer),
            out_shape=shape_of((tokens, BLK), BF),
            in_specs=[VM, HB, VM],
            out_specs=VM,
            scratch_shapes=[
                pltpu.VMEM((3, tokens, BLK), BF),
                pltpu.VMEM((3, D, BLK), BF),
                pltpu.SemaphoreType.DMA((3,)),
            ],
            compiler_params=params(16),
            cost_estimate=cost(3.0),
        )(normed, weights, bias)

    def attend_far(layer, normed, hidden, contexts, here, there, heights):
        return pl.pallas_call(
            partial(attend_far_kernel, layer),
            out_shape=[wide, wide] + [shape_of((height, D), BF) for height in heights],
            in_specs=[SM] + [VM] * 6 + [HB] * 2 + [VM] * 8,
            out_specs=[VM] * (2 + len(heights)),
            scratch_shapes=[
                pltpu.VMEM((2, 3, tokens, BLK), BF),
                pltpu.VMEM((2, tokens, BLK), BF),
                pltpu.VMEM((tokens, D), F32),
                pltpu.VMEM((tokens, D), BF),
                pltpu.VMEM((2 * BLK, D), BF),
                pltpu.SemaphoreType.DMA((2,)),
            ],
            compiler_params=params(20),
            cost_estimate=cost(6.5),
        )(
            place,
            normed,
            bias,
            hidden,
            frozen_gains,
            *contexts,
            frozen_output,
            near_output,
            *here,
            *there,
        )

    def finish(gain_at, hidden, total, came):
        count = 1 if gain_at is None else 2
        return pl.pallas_call(
            partial(finish_kernel, gain_at, len(came)),
            out_shape=[wide] * count,
            in_specs=[VM] * (3 + len(came)),
            out_specs=[VM] * count,
            compiler_params=params(12),
            cost_estimate=cost(1.0),
        )(hidden, total, frozen_gains, *came)

    def feed_own(layer, normed):
        return pl.pallas_call(
            partial(feed_kernel, layer, len(normed)),
            out_shape=sums,
            in_specs=[VM] * (len(normed) + 2),
            out_specs=VM,
            compiler_params=params(12),
            cost_estimate=cost(3.0),
        )(*normed, frozen_expand, frozen_reduce)

    def feed_far(sets, totals, parts, shapes):
        flat = [array for arrays in sets for array in arrays]
        outs = [shape for group in shapes for shape in group]
        return pl.pallas_call(
            partial(feed_far_kernel, [len(a) for a in sets], [len(g) for g in shapes]),
            out_shape=outs,
            in_specs=[VM] * (len(flat) + len(totals) + len(parts)),
            out_specs=[VM] * len(outs),
            compiler_params=params(16),
            cost_estimate=cost(1.0 * len(sets) * len(parts)),
        )(*flat, *totals, *parts)

    def near_all(arrays):
        return [near(array) for array in arrays]

    a0x, near_attend = x(attend_zero), near(frozen_attend)
    side = double(side_own, swap(side_own, "batch", 4))
    near_own, near_output = near(chip_own), near(frozen_output)

    a0x, near_attend, near_own, near_output, chip_far, side = join(
        a0x, near_attend, near_own, near_output, chip_far, side
    )
    far, a0y, a0z, a0x_near, side_came = x(chip_far), y(a0x), z(a0x), near(a0x), z(side)

    far, a0y, a0z, a0x_near, feed_zero, side, side_came = join(
        far, a0y, a0z, a0x_near, feed_zero, side, side_came
    )
    side = double(side, side_came)
    far_near, f0x, a0w, a0y_near, a0z_near = (
        near(far), x(feed_zero), y(a0z), near(a0y), near(a0z),
    )
    hidden, normed = pl.pallas_call(
        assemble_kernel,
        out_shape=[wide] * 2,
        in_specs=[SM] + [VM] * 5,
        out_specs=[VM] * 2,
        compiler_params=params(16),
        cost_estimate=cost(2.0),
    )(place, chip_own, near_own, far, far_near, frozen_gains)
    context = attend_own(0, normed, frozen_attend)

    context, normed, a0w, a0y_near, a0z_near, side = join(
        context, normed, a0w, a0y_near, a0z_near, side
    )
    a0w_near, side_came = near(a0w), y(side)
    contexts = (context, attend_own(0, normed, near_attend))
    here, there = (a0x, a0y, a0z, a0w), (a0x_near, a0y_near, a0z_near, a0w_near)
    halves = split_rows(tokens, 2)
    mid, normed, *sent = attend_far(0, normed, hidden, contexts, here, there, halves)

    mid, normed, *sent, f0x, attend_one, side, side_came = join(
        mid, normed, *sent, f0x, attend_one, side, side_came
    )
    a1x, f0y, f0z, other = x(attend_one), y(f0x), z(f0x), near_all(sent)
    side = double(side, side_came)
    total = feed_own(0, [normed])
    other_total = feed_own(0, other)

    total, other_total, a1x, attend_other, side = join(
        total, other_total, a1x, attend_other, side
    )
    a1z, a1x_near, side_came = x(attend_other), near(a1x), x(side)

    f0y, f0z, a1x, a1x_near, feed_one = join(f0y, f0z, a1x, a1x_near, feed_one)
    f1x, a1y, f0w = x(feed_one), y(a1x), z(f0y)
    total, other_total = feed_far(
        ([normed], other), (total, other_total), (f0x, f0y, f0z), ([sums], [sums])
    )

    total, other_total, a1y, a1z, side, side_came = join(
        total, other_total, a1y, a1z, side, side_came
    )
    a1w, a1y_near, a1z_near = y(a1z), near(a1y), near(a1z)
    side = double(side, side_came)

    f0w, a1w, a1y_near, a1z_near = join(f0w, a1w, a1y_near, a1z_near)
    a1w_near = near(a1w)
    thirds = [shape_of((height, D), BF) for height in split_rows(tokens, 3)]
    came = near_all(feed_far([other], [other_total], [f0w], [thirds]))
    total = feed_far([[normed]], [total], [f0w], [[sums]])[0]
    hidden, normed = finish((1, 0), mid, total, came)
    taps = [hidden]
    f1x, feed_other, normed, side = join(f1x, feed_other, normed, side)
    f1w, f1y, f1z = x(feed_other), y(f1x), z(f1x)
    side = double(side, near(side))
    contexts = [attend_own(1, normed, array) for array in (frozen_attend, near_attend)]
    side_outs = side_layer(hidden, side)
    here, there = (a1x, a1y, a1z, a1w), (a1x_near, a1y_near, a1z_near, a1w_near)
    mid, normed, *sent = attend_far(1, normed, hidden, contexts, here, there, halves)
    other = near_all(sent)
    total = feed_own(1, [normed])
    other_total = feed_own(1, other)

    total, other_total, f1w, f1y, f1z, *side_outs = join(
        total, other_total, f1w, f1y, f1z, *side_outs
    )
    parts = (f1x, f1w, f1y, f1z)
    came = near_all(feed_far([other], [other_total], parts, [thirds]))
    total = feed_far([[normed]], [total], parts, [[sums]])[0]
    taps.append(finish(None, mid, total, came)[0])
    return (taps, side, side_outs)


def split_attend(normed, w_attend, w_output, same_seg):
    col_count = w_attend.shape[2]
    projected = jnp.einsum(
        "rtd,jdc->jrtc", normed, w_attend, preferred_element_type=jnp.float32
    ).astype(jnp.bfloat16)
    head_shape = normed.shape[:2] + (col_count // HEAD_DIM, HEAD_DIM)
    queries = projected[0].reshape(head_shape)
    key_rows = projected[1].reshape(head_shape)
    value_rows = projected[2].reshape(head_shape)
    scores = jnp.einsum(
        "rqhc,rkhc->rhqk", queries, key_rows, preferred_element_type=jnp.float32
    ) * HEAD_DIM ** (-0.5)
    scores = jnp.where(same_seg[:, None], scores, MASKED)
    shares = jax.nn.softmax(scores, axis=-1).astype(jnp.bfloat16)
    context = jnp.einsum("rhqk,rkhc->rqhc", shares, value_rows, preferred_element_type=jnp.float32)
    context = context.astype(jnp.bfloat16).reshape(normed.shape[:2] + (col_count,))
    return jnp.einsum("rtc,cd->rtd", context, w_output, preferred_element_type=jnp.float32)


def split_feed(normed, w_expand, w_reduce):
    inner = jax.nn.gelu(
        jnp.einsum("rtd,df->rtf", normed, w_expand, preferred_element_type=jnp.float32)
    ).astype(jnp.bfloat16)
    return jnp.einsum("rtf,fd->rtd", inner, w_reduce, preferred_element_type=jnp.float32)


def split_sublayer(hidden, gains, work):
    whole = lax.all_gather(hidden, "head", axis=2, tiled=True)
    normed = root_norm(whole.astype(jnp.float32), gains).astype(jnp.bfloat16)
    summed = lax.psum_scatter(
        work(normed).astype(jnp.bfloat16), "head", scatter_dimension=2, tiled=True
    ).astype(jnp.float32)
    return (hidden.astype(jnp.float32) + summed).astype(jnp.bfloat16)


def backbone_split(
    frozen_input, frozen_attend, frozen_output, frozen_expand, frozen_reduce, frozen_gains, lengths
):
    taps = []
    same_all, _ = segments(lengths)
    hidden = frozen_input
    for layer in range(L):
        hidden = split_sublayer(
            hidden,
            frozen_gains[layer, 0],
            partial(
                split_attend,
                w_attend=frozen_attend[layer],
                w_output=frozen_output[layer],
                same_seg=same_all,
            ),
        )
        hidden = split_sublayer(
            hidden,
            frozen_gains[layer, 1],
            partial(split_feed, w_expand=frozen_expand[layer], w_reduce=frozen_reduce[layer]),
        )
        tapped = lax.all_to_all(hidden, "head", split_axis=0, concat_axis=2, tiled=True)
        taps.append(tapped.reshape(-1, D))
    return taps


def shards(
    frozen_input,
    frozen_attend,
    frozen_output,
    frozen_expand,
    frozen_reduce,
    frozen_gains,
    lengths,
    side_input,
    cotangent,
    attend_master,
    attend_moment,
    attend_square,
    feed_master,
    feed_moment,
    feed_square,
    down_master,
    down_moment,
    down_square,
    gains_master,
    gains_moment,
    gains_square,
):
    head_count, batch_count = lax.axis_size("head"), lax.axis_size("batch")
    tuned = head_count == 4 and batch_count == 8
    head_at, batch_at = lax.axis_index("head"), lax.axis_index("batch")
    own_rows = lengths.shape[0] // head_count
    place = jnp.stack(
        [
            head_at,
            batch_at % 4,
            head_at % 2,
            head_at // 2 % 2,
            batch_at % 2,
            batch_at // 2 % 2,
            batch_at // 4 % 2,
            batch_at * head_count + head_at,
            jnp.zeros_like(head_at),
            gathered_at(batch_at * head_count + head_at) if tuned else jnp.zeros_like(head_at),
        ]
    ).astype(jnp.int32)
    tokens = own_rows * ROW
    state_in = side_input.reshape(tokens, S)
    frozen = (frozen_attend, frozen_output, frozen_expand, frozen_reduce, frozen_gains)
    masters = (attend_master, feed_master, down_master)
    given = (lengths, cotangent.reshape(tokens, S))
    if tuned:
        attend_zero = pack_first(place, frozen_attend, frozen_output)
        attend_zero, *given = join(attend_zero, *given)
    bias, grad_seed, *side_own = prepare(given[0], place, given[1], masters, tuned)
    if tuned:
        taps, whole, (*saved, state) = backbone_rows(
            place,
            frozen_input,
            *frozen,
            attend_zero,
            bias,
            *side_own,
            lambda tap, whole: side_first(place, tap, whole, state_in, gains_master, bias),
        )
    else:
        mats, feeds, downs = (
            lax.all_gather(array.astype(BF), ("batch", "head"), axis=0, tiled=True)
            for array in masters
        )
        feeds = feeds.reshape(PLACES, -1, SF // S, S).transpose(0, 2, 1, 3)
        whole = jnp.concatenate(
            [array.reshape(PLACES, -1, S) for array in (mats, feeds, downs)], axis=1
        )
        whole = whole.reshape((2,) * 5 + whole.shape[1:]).transpose(4, 3, 2, 1, 0, 5, 6)
        whole = whole.reshape(PLACES, -1, S)
        taps = backbone_split(frozen_input, *frozen, lengths)
        *saved, state = side_first(place, taps[0], whole, state_in, gains_master, bias)
    result, input_grad, *sums = side_last(
        PLACES if tuned else 0,
        place,
        *taps,
        whole,
        state_in,
        state,
        grad_seed,
        gains_master,
        bias,
        saved,
    )
    result = result.reshape(cotangent.shape)
    input_grad = input_grad.reshape(cotangent.shape)
    states = (
        attend_master,
        attend_moment,
        attend_square,
        feed_master,
        feed_moment,
        feed_square,
        down_master,
        down_moment,
        down_square,
        gains_master,
        gains_moment,
        gains_square,
    )
    if tuned:
        kept, sent, small = sums
        small = small + swap(small, "batch", 4)
        kept, came = scatter_sums(place, kept, sent)
        total, small = tally(place, kept, came, small)
        for axis, bit in (("head", 1), ("head", 2), ("batch", 1), ("batch", 2)):
            small = small + swap(small, axis, bit)
        grad_norm, *rest = update(total, small, states)
        return (result, input_grad, grad_norm.reshape(()), *rest)
    grads = lax.psum(tuple(sums), ("batch", "head"))
    grad_norm = jnp.sqrt(sum(jnp.sum(grad * grad) for grad in grads))
    clip = jnp.minimum(1.0, THRESHOLD / grad_norm)
    member = lax.axis_index(("batch", "head"))
    outs = []
    for at, grad in enumerate(grads):
        owned = states[3 * at : 3 * at + 3]
        if at < 3:
            height = owned[0].shape[0]
            grad = lax.dynamic_slice_in_dim(grad, member * height, height, 0)
        rate, decay = (RATE_MATRIX, WEIGHT_DECAY) if at < 3 else (RATE_SMALL, 0.0)
        new = adamw(*owned, grad, clip, rate, decay)
        outs.extend(new)
        if at < 3:
            outs.append(new[0].astype(BF))
    return (result, input_grad, grad_norm, *outs)


def solution(mesh):
    row_split = P(("batch", "head"), None)
    cube_split = P(("batch", "head"), None, None)
    return jax.shard_map(
        shards,
        mesh=mesh,
        in_specs=(
            P("batch", None, "head"),
            P(None, None, None, "head"),
            P(None, "head", None),
            P(None, None, "head"),
            P(None, "head", None),
            P(),
            P("batch", None),
            cube_split,
            cube_split,
        )
        + (row_split,) * 9
        + (P(),) * 3,
        out_specs=(cube_split, cube_split, P()) + (row_split,) * 12 + (P(),) * 3,
        check_vma=False,
    )
```

```python
from functools import partial

import jax
import jax.numpy as jnp
from jax import lax
from jax.experimental import pallas as pl
from jax.experimental.pallas import tpu as pltpu
from jax.sharding import PartitionSpec as P

D = 1024
HEAD_DIM = 64
S = 128
SIDE_HD = 8
SF = 512
L = 2
ROW = 128
STEP = 10


NORM_EPS = 1e-06
THRESHOLD = 1.0
BETA_ONE = 0.9
BETA_TWO = 0.999
ADAM_EPS = 1e-08
RATE_MATRIX = 0.12
RATE_SMALL = 0.5
WEIGHT_DECAY = 0.01
MASKED = -1e30

BF = jnp.bfloat16
F32 = jnp.float32
BLK = 256
PLACES = 32
MIB = 2**20

VM = pl.BlockSpec(memory_space=pltpu.VMEM)
SM = pl.BlockSpec(memory_space=pltpu.SMEM)
HB = pl.BlockSpec(memory_space=pltpu.HBM)


def shape_of(dims, kind):
    return jax.ShapeDtypeStruct(dims, kind)


def params(mib):
    return pltpu.CompilerParams(vmem_limit_bytes=mib * MIB)


def cost(micros):
    return pl.CostEstimate(flops=int(micros * 1e6), bytes_accessed=0, transcendentals=0)


def gelu(values):
    squared = values * values
    half = 0.5 * values
    bent = jnp.tanh(values * (0.7978845608028654 + 0.7978845608028654 * 0.044715 * squared))
    return half + half * bent


class Fetch:
    def __init__(self, sems):
        self.sems, self.items = sems, []

    def start(self, source, target):
        item = pltpu.make_async_copy(source, target, self.sems.at[len(self.items)])
        self.items.append(item)
        item.start()
        return item


def nn(a, b):
    return lax.dot_general(a, b, (((1,), (0,)), ((), ())), preferred_element_type=F32)


def nt(a, b):
    return lax.dot_general(a, b, (((1,), (1,)), ((), ())), preferred_element_type=F32)


def norm_scale(values):
    return lax.rsqrt(jnp.mean(values * values, axis=-1, keepdims=True) + NORM_EPS)


def root_norm(values, gains):
    return values * norm_scale(values) * gains


def segments(lengths):
    sent_ends = jnp.cumsum(lengths, axis=-1)
    kept_flag = sent_ends <= ROW
    places = jnp.arange(ROW, dtype=jnp.int32)
    labels = jnp.sum(
        (kept_flag[:, None, :] & (sent_ends[:, None, :] <= places[None, :, None])).astype(
            jnp.int32
        ),
        axis=-1,
    )
    filled = jnp.sum(jnp.where(kept_flag, lengths, 0), axis=-1)
    real_tok = (places[None, :] < filled[:, None]).astype(jnp.float32)
    return (labels[:, :, None] == labels[:, None, :], real_tok)


def side_by_side(rows2):
    return jnp.concatenate([rows2[:ROW], rows2[ROW:]], axis=1)


def block_diagonal(rows2):
    blank = jnp.zeros((ROW, ROW), rows2.dtype)
    top = jnp.concatenate([rows2[:ROW], blank], axis=1)
    low = jnp.concatenate([blank, rows2[ROW:]], axis=1)
    return jnp.concatenate([top, low], axis=0)


def head_masks(head_dim, first):
    lanes = lax.broadcasted_iota(jnp.int32, (ROW, 2 * ROW), 1) % ROW // head_dim
    return (lanes == first, lanes == first + 1)


def stack_heads(wide, masks):
    blank = jnp.zeros_like(wide)
    return jnp.concatenate(
        [jnp.where(masks[0], wide, blank), jnp.where(masks[1], wide, blank)], axis=0
    )


def shares_of(scores, bias, scale):
    scores = scores.reshape(2, ROW, 2 * ROW) + bias[None]
    highest = jnp.max(scores, axis=1, keepdims=True)
    weights = jnp.exp2((scores - highest) * (scale * 1.4426950408889634))
    return weights * (1.0 / jnp.sum(weights, axis=1, keepdims=True))


def head_rows(flipped, count):
    rows = lax.broadcasted_iota(jnp.int32, flipped.shape, 0)
    blank = jnp.zeros_like(flipped)
    return jnp.concatenate(
        [jnp.where(rows < count, flipped, blank), jnp.where(rows >= count, flipped, blank)], axis=1
    )


def diagonal_of(flipped, pair):
    return block_diagonal(jnp.concatenate([flipped[2 * pair], flipped[2 * pair + 1]], axis=0))


def flip(values):
    return values.astype(F32).T


def backbone_heads(proj, bias_ref, context_ref):
    masks = head_masks(HEAD_DIM, 0)
    spots = [
        (pair, slice(pair * 2 * ROW, (pair + 1) * 2 * ROW), slice(lane * ROW, (lane + 1) * ROW))
        for pair in range(proj.shape[1] // (2 * ROW))
        for lane in range(proj.shape[2] // ROW)
    ]
    scores = []
    for _, rows, lanes in spots:
        queries = proj[0, rows, lanes]
        flipped = jnp.concatenate(
            [flip(queries[at * ROW : (at + 1) * ROW]).astype(BF) for at in range(2)], axis=0
        )
        keys = stack_heads(side_by_side(proj[1, rows, lanes]), masks)
        scores.append(nn(keys, block_diagonal(flipped)))
    shares = [
        shares_of(score, bias_ref[pair], HEAD_DIM**-0.5).astype(BF).reshape(2 * ROW, 2 * ROW)
        for score, (pair, _, _) in zip(scores, spots)
    ]
    outs = []
    for share, (_, rows, lanes) in zip(shares, spots):
        values = proj[2, rows, lanes]
        for at in range(2):
            flipped = flip(values[at * ROW : (at + 1) * ROW]).astype(BF)
            out = nn(head_rows(flipped, HEAD_DIM), share[:, at * ROW : (at + 1) * ROW])
            outs.append(out.T.astype(BF))
    for index, (_, rows, lanes) in enumerate(spots):
        for at in range(2):
            start = rows.start + at * ROW
            context_ref[start : start + ROW, lanes] = outs[2 * index + at]


def assemble_kernel(place, own, near, far, far_near, gains, hidden_ref, normed_ref):
    rows = own.shape[0] // 2
    mine = pl.ds(place[2] * rows, rows)
    for step, piece in enumerate((own, near, far, far_near)):
        spot = pl.multiple_of((place[0] ^ step) * BLK, BLK)
        hidden_ref[:, pl.ds(spot, BLK)] = piece[mine].reshape(rows * ROW, BLK)
    normed_ref[...] = root_norm(hidden_ref[...].astype(F32), gains[0, 0:1]).astype(BF)


def split_rows(total, count):
    heights = [(total // count + 15) // 16 * 16] * (count - 1)
    return heights + [total - sum(heights)]


def load_rows(refs):
    return refs[0][...] if len(refs) == 1 else jnp.concatenate([ref[...] for ref in refs], axis=0)


def store_rows(refs, columns, value):
    start = 0
    for ref in refs:
        ref[:, columns] = value[start : start + ref.shape[0]].astype(ref.dtype)
        start += ref.shape[0]


def attend_kernel(layer, normed, weights_a, weights_b, bias, context_a, context_b, proj):
    for slot, weights in enumerate((weights_a, weights_b)):
        for at in range(3):
            proj[slot, at] = nn(normed[...], weights[layer, at]).astype(BF)
    for slot, context in enumerate((context_a, context_b)):
        backbone_heads(proj.at[slot], bias, context)


def attend_far_kernel(
    layer, place, normed, bias, hidden, gains, context_a, context_b, out_a, out_b, *rest
):
    parts, (mid_ref, normed_ref, *sent) = rest[:8], rest[8:-6]
    proj, context, total, turned, held, sems = rest[-6:]
    fetch = Fetch(sems)
    waits = [
        fetch.start(source.at[layer], held.at[pl.ds(at * BLK, BLK)])
        for at, source in enumerate((out_a, out_b))
    ]
    spots = [pl.ds(pl.multiple_of((place[1] ^ step) * BLK, BLK), BLK) for step in range(4)]
    for step, spot in enumerate(spots):
        turned[:, step * BLK : (step + 1) * BLK] = normed[:, spot]
    for slot, group in enumerate((parts[:4], parts[4:])):
        for at in range(3):
            weights = jnp.concatenate([part[at] for part in group], axis=0)
            proj[slot, at] = nn(turned[...], weights).astype(BF)
    for slot in range(2):
        backbone_heads(proj.at[slot], bias, context.at[slot])
    for item in waits:
        item.wait()
    both = jnp.concatenate([context_a[...], context_b[...], context[0], context[1]], axis=1)
    for step, spot in enumerate(spots):
        weights = jnp.concatenate([held[:, spot], parts[step][3], parts[4 + step][3]], axis=0)
        total[:, spot] = hidden[:, spot].astype(F32) + nn(both, weights)
    mid = total[...].astype(BF)
    mid_ref[...] = mid
    normed_now = root_norm(mid.astype(F32), gains[layer, 1:2])
    store_rows((normed_ref,), slice(None), normed_now)
    store_rows(sent, slice(None), normed_now)


def finish_kernel(gain_at, count, hidden, total, gains, *refs):
    outs = refs[count:]
    came = load_rows(refs[:count]).astype(F32)
    value = (hidden[...].astype(F32) + (total[...] + came)).astype(BF)
    outs[0][...] = value
    if gain_at is not None:
        layer, at = gain_at
        outs[1][...] = root_norm(value.astype(F32), gains[layer, at : at + 1]).astype(BF)


def feed_kernel(layer, count, *refs):
    normed, (expand, reduce, total_ref) = refs[:count], refs[count:]
    values = load_rows(normed)
    for at in range(expand.shape[2] // (2 * BLK)):
        units = slice(at * 2 * BLK, (at + 1) * 2 * BLK)
        inner = gelu(nn(values, expand[layer, :, units])).astype(BF)
        term = nn(inner, reduce[layer, units, :])
        if at == 0:
            total_ref[...] = term
        else:
            total_ref[...] += term


def feed_far_kernel(counts, layout, *refs):
    refs = list(refs)

    def take(count):
        taken = refs[:count]
        del refs[:count]
        return taken

    sets = [take(count) for count in counts]
    totals = take(len(counts))
    outs = [refs[len(refs) - sum(layout) :][sum(layout[:at]) : sum(layout[: at + 1])] for at in range(len(counts))]
    parts = refs[: len(refs) - sum(layout)]
    for normed, total, out in zip(sets, totals, outs):
        values = load_rows(normed)
        inners = [gelu(nn(values, part[0:4].reshape(D, BLK))).astype(BF) for part in parts]
        inner = jnp.concatenate(inners, axis=1)
        for at in range(4):
            weights = jnp.concatenate([part[4 + at] for part in parts], axis=0)
            columns = slice(at * BLK, (at + 1) * BLK)
            store_rows(out, columns, total[:, columns] + nn(inner, weights))


def pack_first_kernel(place, attend, output, attend_part, sems):
    fetch = Fetch(sems)
    spot = pl.ds(pl.multiple_of(place[1] * BLK, BLK), BLK)
    for at in range(3):
        fetch.start(attend.at[0, at, spot, :], attend_part.at[at])
    fetch.start(output.at[0, :, spot], attend_part.at[3])
    for item in fetch.items:
        item.wait()


def pack_first(place, attend, output):
    return pl.pallas_call(
        pack_first_kernel,
        out_shape=shape_of((4, BLK, BLK), BF),
        in_specs=[SM] + [HB] * 2,
        out_specs=VM,
        scratch_shapes=[pltpu.SemaphoreType.DMA((4,))],
        compiler_params=params(57),
        cost_estimate=cost(1.0),
    )(place, attend, output)


def split_chip_kernel(place, hidden, chip_far, chip_own, sems):
    fetch = Fetch(sems)
    rows = chip_own.shape[0]
    fetch.start(hidden.at[pl.ds((1 - place[3]) * rows, rows)], chip_far)
    fetch.start(hidden.at[pl.ds(place[3] * rows, rows)], chip_own)
    for item in fetch.items:
        item.wait()


def split_chip(place, hidden):
    half = (hidden.shape[0] // 2,) + hidden.shape[1:]
    return pl.pallas_call(
        split_chip_kernel,
        out_shape=[shape_of(half, BF)] * 2,
        in_specs=[SM, HB],
        out_specs=[VM] * 2,
        scratch_shapes=[pltpu.SemaphoreType.DMA((2,))],
        compiler_params=params(4),
        cost_estimate=cost(1.0),
    )(place, hidden)


def pack_kernel(place, attend, output, expand, reduce, attend_part, attend_other, *rest):
    feed_targets, sems = rest[:-1], rest[-1]
    fetch = Fetch(sems)
    spot = pl.ds(pl.multiple_of(place[1] * BLK, BLK), BLK)
    last = pl.ds(pl.multiple_of((place[1] ^ 3) * BLK, BLK), BLK)
    for layer, units, target in zip((0, 1, 1), (spot, spot, last), feed_targets):
        for at in range(4):
            rows = pl.ds(at * BLK, BLK)
            fetch.start(expand.at[layer, rows, units], target.at[at])
            fetch.start(reduce.at[layer, units, rows], target.at[4 + at])
    other = pl.ds(pl.multiple_of((place[1] ^ 2) * BLK, BLK), BLK)
    for rows, target in ((spot, attend_part), (other, attend_other)):
        for at in range(3):
            fetch.start(attend.at[1, at, rows, :], target.at[at])
        fetch.start(output.at[1, :, rows], target.at[3])
    for item in fetch.items:
        item.wait()


def pack(place, attend, output, expand, reduce):
    return pl.pallas_call(
        pack_kernel,
        out_shape=[shape_of((4, BLK, BLK), BF)] * 2 + [shape_of((8, BLK, BLK), BF)] * 3,
        in_specs=[SM] + [HB] * 4,
        out_specs=[VM] * 5,
        scratch_shapes=[pltpu.SemaphoreType.DMA((32,))],
        compiler_params=params(57),
        cost_estimate=cost(2.0),
    )(place, attend, output, expand, reduce)


def prepare_kernel(lengths, place, cotangent, *rest):
    masters, (bias_ref, seed_ref, *packed) = rest[:3], rest[3:]
    rows = cotangent.shape[0] // ROW
    deep = lax.broadcasted_iota(jnp.int32, (ROW, ROW), 0)
    across = lax.broadcasted_iota(jnp.int32, (ROW, ROW), 1)
    for row in range(rows):
        end = jnp.int32(0)
        filled = jnp.int32(0)
        deep_label = jnp.zeros((ROW, ROW), jnp.int32)
        across_label = jnp.zeros((ROW, ROW), jnp.int32)
        for slot in range(lengths.shape[0]):
            length = lengths[slot, place[0] * rows + row]
            end = end + length
            kept = end <= ROW
            filled = filled + jnp.where(kept, length, 0)
            start = jnp.where(kept, end, ROW)
            deep_label += (deep >= start).astype(jnp.int32)
            across_label += (across >= start).astype(jnp.int32)
        pair, at = row // 2, row % 2
        bias_ref[pair, :, at * ROW : (at + 1) * ROW] = jnp.where(
            deep_label == across_label, 0.0, MASKED
        )
        spot = slice(row * ROW, (row + 1) * ROW)
        seed_ref[spot] = jnp.where(deep < filled, cotangent[spot], 0.0)
    if packed:
        base = 0
        for master in masters:
            height, width = master.shape
            for column in range(width // S):
                packed[0][0, base : base + height] = master[:, column * S : (column + 1) * S].astype(BF)
                base += height


def prepare(lengths, place, cotangent, masters, packed):
    tokens = cotangent.shape[0]
    shapes = [shape_of((tokens // ROW // 2, ROW, 2 * ROW), F32), shape_of((tokens, S), F32)]
    if packed:
        shapes.append(shape_of((1, sum(master.size for master in masters) // S, S), BF))
    return pl.pallas_call(
        prepare_kernel,
        out_shape=shapes,
        in_specs=[SM, SM] + [VM] * 4,
        out_specs=[VM] * len(shapes),
        compiler_params=params(57),
        cost_estimate=cost(1.5),
    )(lengths.T, place, cotangent, *masters)


TURNS = S // SIDE_HD // 2
GROUP = 8


def spot_of(index, size):
    if isinstance(index, int):
        return slice(index * size, (index + 1) * size)
    return pl.ds(pl.multiple_of(index * size, size), size)


def head_spot(turn):
    return spot_of(turn, 2 * SIDE_HD)


def repeat(count, step, unrolled):
    if unrolled:
        for index in range(count):
            step(index, 0)
    else:
        lax.fori_loop(0, count, step, 0)


def saved_shapes(tokens):
    return {
        "tapped": ((tokens, S), F32),
        "mixed": ((tokens, S), F32),
        "middle": ((tokens, S), F32),
        "queries": ((tokens, S), BF),
        "keys": ((tokens, S), BF),
        "values": ((tokens, S), BF),
        "context": ((tokens // ROW, S, ROW), F32),
        "shares": ((tokens // (2 * ROW) * TURNS, 2 * ROW, 2 * ROW), BF),
    }


def flip_rows(source, target):
    for at in range(target.shape[0]):
        target[at] = flip(source[at * ROW : (at + 1) * ROW]).astype(target.dtype)


def rows_side_by_side(source):
    return jnp.concatenate([source[at] for at in range(source.shape[0])], axis=1)


def query_rows(flipped, first, spot):
    top, low = flipped[first, spot], flipped[first + 1, spot]
    blank = jnp.zeros_like(top)
    return jnp.concatenate(
        [jnp.concatenate([top, blank], axis=1), jnp.concatenate([blank, low], axis=1)], axis=0
    )


def key_rows(flipped, first, spot):
    return jnp.concatenate(
        [head_rows(flipped[first + at, spot], SIDE_HD) for at in range(2)], axis=0
    )


def gathered_at(device):
    order = (4, 3, 2, 1, 0)
    return sum((device >> bit & 1) << at for at, bit in enumerate(order))


def matrix_loader(place, whole, places):
    heights = (L * 4 * S // places, L * 2 * S // places, L * D // places)
    feed_base = heights[0]
    down_base = feed_base + heights[1] * (SF // S)

    def rows(first, total, base, height):
        start = first // height
        return jnp.concatenate(
            [
                whole[gathered_at(start + step) ^ place[9], base : base + height]
                for step in range(total // height)
            ],
            axis=0,
        )

    def load(layer, mats, feeds, down=None):
        for at in range(4):
            mats[at] = rows((layer * 4 + at) * S, S, 0, heights[0])
        for at in range(2):
            for column in range(SF // S):
                feeds[at, :, column * S : (column + 1) * S] = rows(
                    (layer * 2 + at) * S, S, feed_base + column * heights[1], heights[1]
                )
        if down is not None:
            down[...] = rows(layer * D, D, down_base, heights[2])

    return load


def side_forward(
    tap_source, down, state, mats, feeds, smalls, bias_ref, saved, flips, result_ref, unrolled
):
    tokens = state.shape[0]
    gating = jax.nn.sigmoid(smalls[2:3])
    tapped = nn(tap_source, down)
    mixed = gating * tapped + (1.0 - gating) * state
    saved["tapped"][...] = tapped
    saved["mixed"][...] = mixed
    normed = (mixed * norm_scale(mixed) * smalls[0:1]).astype(BF)
    for at, name in enumerate(("queries", "keys", "values")):
        saved[name][...] = nn(normed, mats[at]).astype(BF)
    flip_rows(saved["values"], flips.at[0])
    flip_rows(saved["queries"], flips.at[1])
    groups = TURNS // GROUP

    def step(index, carry):
        pair, first = index // groups, index % groups * GROUP
        rows = spot_of(pair, 2 * ROW)
        keys = side_by_side(saved["keys"][rows])
        stacks = [stack_heads(keys, head_masks(SIDE_HD, 2 * (first + at))) for at in range(GROUP)]
        scores = nn(jnp.concatenate(stacks, axis=0), diagonal_of(flips.at[1], pair))
        bias = bias_ref[pair]
        spots = [head_spot(first + at) for at in range(GROUP)]
        lefts = [key_rows(flips.at[0], 2 * pair, spot) for spot in spots]
        shares, outs = [], []
        for at in range(GROUP):
            own = shares_of(scores[at * 2 * ROW : (at + 1) * 2 * ROW], bias, SIDE_HD**-0.5)
            shares.append(own.astype(BF).reshape(2 * ROW, 2 * ROW))
            outs.append(nn(lefts[at], shares[-1]))
        for at, spot in enumerate(spots):
            saved["shares"][pair * TURNS + first + at] = shares[at]
            saved["context"][2 * pair, spot] = outs[at][: 2 * SIDE_HD, :ROW]
            saved["context"][2 * pair + 1, spot] = outs[at][2 * SIDE_HD :, ROW:]
        return carry

    repeat(tokens // (2 * ROW) * groups, step, unrolled)
    context = jnp.concatenate(
        [saved["context"][at].T.astype(BF) for at in range(tokens // ROW)], axis=0
    )
    middle = mixed + nn(context, mats[3])
    saved["middle"][...] = middle
    normed_two = (middle * norm_scale(middle) * smalls[1:2]).astype(BF)
    active = gelu(nn(normed_two, feeds[0])).astype(BF)
    result_ref[...] = middle + nt(active, feeds[1])


def gelu_parts(inner):
    root = 0.7978845608028654
    squared = inner * inner
    bent = jnp.tanh(root * inner * (1.0 + 0.044715 * squared))
    half = 0.5 * (1.0 + bent)
    slope = half + 0.5 * inner * (1.0 - bent * bent) * (root * (1.0 + 3.0 * 0.044715 * squared))
    return (inner * half, slope)


def norm_back(values, scale, gains, grad_normed):
    weighted = grad_normed * gains
    grad_values = scale * weighted - values * scale**3 * jnp.mean(
        weighted * values, axis=-1, keepdims=True
    )
    return (grad_values, jnp.sum(grad_normed * values * scale, axis=0, keepdims=True))


def side_backward(tap_source, state, grad_out, mats, feeds, smalls, bias_ref, saved, work, put):
    flips, grad_flips, means = work
    tokens = grad_out.shape[0]
    pairs = tokens // (2 * ROW)
    middle = saved["middle"][...]
    second_scale = norm_scale(middle)
    normed_two = (middle * second_scale * smalls[1:2]).astype(BF)
    active, slope = gelu_parts(nn(normed_two, feeds[0]))
    grad_outer = grad_out.astype(BF)
    put("feed", 1, nn(flip(grad_outer).astype(BF), active.astype(BF)))
    grad_inner = (nn(grad_outer, feeds[1]) * slope).astype(BF)
    put("feed", 0, nn(flip(normed_two).astype(BF), grad_inner))
    grad_middle, grad_gain_two = norm_back(
        middle, second_scale, smalls[1:2], nt(grad_inner, feeds[0])
    )
    put("gain", 1, grad_gain_two)
    grad_middle = grad_middle + grad_out
    grad_branch = grad_middle.astype(BF)
    context_flip = rows_side_by_side(saved["context"])
    put("attend", 3, nn(context_flip.astype(BF), grad_branch))
    grad_context = nt(mats[3], grad_branch).astype(BF)
    for at in range(tokens // ROW):
        flips[2, at] = grad_context[:, at * ROW : (at + 1) * ROW]
    flip_rows(saved["queries"], flips.at[0])
    flip_rows(saved["keys"], flips.at[1])
    products = (grad_context.astype(F32) * context_flip).reshape(S // SIDE_HD, SIDE_HD, tokens)
    sums = jnp.sum(products, axis=1)
    for pair in range(pairs):
        for head in range(TURNS):
            means[pair * TURNS + head] = sums[
                2 * head : 2 * head + 2, pair * 2 * ROW : (pair + 1) * 2 * ROW
            ]

    groups = TURNS // GROUP

    def step(index, carry):
        pair, first = index // groups, index % groups * GROUP
        rows = spot_of(pair, 2 * ROW)
        values = side_by_side(saved["values"][rows])
        stacks = [stack_heads(values, head_masks(SIDE_HD, 2 * (first + at))) for at in range(GROUP)]
        products = nn(jnp.concatenate(stacks, axis=0), diagonal_of(flips.at[2], pair))
        turns = [pair * TURNS + first + at for at in range(GROUP)]
        spots = [head_spot(first + at) for at in range(GROUP)]
        shares = [saved["shares"][turn] for turn in turns]
        centres = [means[turn].reshape(2, 1, 2 * ROW) for turn in turns]
        key_lefts = [key_rows(flips.at[1], 2 * pair, spot) for spot in spots]
        query_lefts = [query_rows(flips.at[0], 2 * pair, spot) for spot in spots]
        grad_lefts = [query_rows(flips.at[2], 2 * pair, spot) for spot in spots]
        upper = lax.broadcasted_iota(jnp.int32, (2 * SIDE_HD, ROW), 0) < SIDE_HD
        outs = []
        for at in range(GROUP):
            grad = products[at * 2 * ROW : (at + 1) * 2 * ROW].reshape(2, ROW, 2 * ROW)
            grad = shares[at].astype(F32).reshape(2, ROW, 2 * ROW) * (grad - centres[at])
            grad = grad.astype(BF).reshape(2 * ROW, 2 * ROW)
            outs.append(
                (
                    nn(key_lefts[at], grad),
                    nt(query_lefts[at], grad),
                    nt(grad_lefts[at], shares[at]),
                )
            )
        for spot, (query_part, *others) in zip(spots, outs):
            grad_flips[0, 2 * pair, spot] = query_part[: 2 * SIDE_HD, :ROW]
            grad_flips[0, 2 * pair + 1, spot] = query_part[2 * SIDE_HD :, ROW:]
            for slot, out in enumerate(others):
                for at in range(2):
                    half = out[at * 2 * SIDE_HD : (at + 1) * 2 * SIDE_HD]
                    grad_flips[1 + slot, 2 * pair + at, spot] = jnp.where(
                        upper, half[:, :ROW], half[:, ROW:]
                    )
        return carry

    repeat(pairs * groups, step, True)
    root = SIDE_HD**-0.5
    mixed = saved["mixed"][...]
    first_scale = norm_scale(mixed)
    normed_flip = flip((mixed * first_scale * smalls[0:1]).astype(BF)).astype(BF)
    grad_normed = None
    for at, factor in enumerate((root, root, None)):
        grad = rows_side_by_side(grad_flips.at[at])
        grad = (grad if factor is None else grad * factor).astype(BF)
        put("attend", at, nt(normed_flip, grad))
        term = nn(mats[at], grad)
        grad_normed = term if grad_normed is None else grad_normed + term
    grad_normed = grad_normed.T
    grad_mixed, grad_gain_one = norm_back(mixed, first_scale, smalls[0:1], grad_normed)
    put("gain", 0, grad_gain_one)
    grad_mixed = grad_mixed + grad_middle
    gating = jax.nn.sigmoid(smalls[2:3])
    grad_tap = (gating * grad_mixed).astype(BF)
    put(
        "gain",
        2,
        jnp.sum(grad_mixed * (saved["tapped"][...] - state), axis=0, keepdims=True)
        * gating
        * (1.0 - gating),
    )
    put("down", 0, nn(flip(grad_tap).astype(BF), tap_source).T)
    return (1.0 - gating) * grad_mixed


MATRICES = [
    pltpu.VMEM((4, S, S), BF),
    pltpu.VMEM((2, S, SF), BF),
    pltpu.VMEM((D, S), BF),
]


def side_first_kernel(place, tap_source, whole, state, smalls, bias, *rest):
    outs, (flips, mats, feeds, down) = rest[:-4], rest[-4:]
    matrix_loader(place, whole, PLACES)(0, mats, feeds, down)
    saved = dict(zip(saved_shapes(state.shape[0]), outs))
    side_forward(
        tap_source[...],
        down[...],
        state[...].astype(F32),
        mats,
        feeds,
        smalls[0:3],
        bias,
        saved,
        flips,
        outs[-1],
        False,
    )


def side_first(place, tap_source, whole, state, smalls, bias):
    tokens = state.shape[0]
    return pl.pallas_call(
        side_first_kernel,
        out_shape=[shape_of(*item) for item in saved_shapes(tokens).values()]
        + [shape_of((tokens, S), F32)],
        in_specs=[SM] + [VM] * 5,
        out_specs=[VM] * (len(saved_shapes(tokens)) + 1),
        scratch_shapes=[pltpu.VMEM((2, tokens // ROW, S, ROW), BF)] + MATRICES,
        compiler_params=params(16),
        cost_estimate=cost(8.0),
    )(place, tap_source, whole, state, smalls, bias)


def side_last_kernel(
    packed,
    place,
    tap_one,
    tap_two,
    whole_in,
    state_in,
    state,
    cotangent,
    smalls,
    bias,
    *rest,
):
    names = saved_shapes(cotangent.shape[0])
    count = len(names)
    saved_one = dict(zip(names, rest[:count]))
    rest = rest[count:]
    result_ref, grad_ref = rest[:2]
    outs = rest[2:5] if packed else rest[2:6]
    rest = rest[len(outs) + 2 :]
    saved_two = dict(zip(names, rest[:count]))
    work = rest[count : count + 3]
    mats, feeds, down = rest[count + 3 : count + 6]
    load = matrix_loader(place, whole_in, PLACES)
    load(1, mats, feeds, down)
    if packed:
        places = outs[0].shape[0] * 2
        widths = (L * 4 * S // places, L * 2 * S // places, L * D // places)
        feed_base = widths[0]
        down_base = feed_base + widths[1] * (SF // S)
        even = place[2] == 0
        outs[2][...] = jnp.zeros_like(outs[2])

    def put_rows(start, base, value):
        kept = jnp.where(even, value[:, 0], value[:, 1])
        sent = jnp.where(even, value[:, 1], value[:, 0])
        spot = (slice(start, start + value.shape[0]), slice(base, base + value.shape[2]))
        outs[0][spot] = kept
        outs[1][spot] = sent.astype(BF)

    def put_at(layer, kind, at, value):
        if not packed:
            target = outs[("attend", "feed", "down", "gain").index(kind)]
            if kind == "gain":
                target[3 * layer + at : 3 * layer + at + 1] = value
            else:
                first = {"attend": (layer * 4 + at) * S, "feed": (layer * 2 + at) * S}.get(
                    kind, layer * D
                )
                target[first : first + value.shape[0]] = value
            return
        if kind == "gain":
            outs[2][8 + 3 * layer + at : 9 + 3 * layer + at] = value
            return
        width = widths[("attend", "feed", "down").index(kind)]
        half = value.shape[0] // width // 2
        if kind == "feed":
            start = (layer * 2 + at) * half
            for column in range(SF // S):
                part = value[:, column * S : (column + 1) * S].reshape(half, 2, width, S)
                put_rows(start, feed_base + column * width, part)
        else:
            base = 0 if kind == "attend" else down_base
            start = (layer * 4 + at) * half if kind == "attend" else layer * half
            put_rows(start, base, value.reshape(half, 2, width, S))

    smalls_one, smalls_two = smalls[0:3], smalls[3:6]
    side_forward(
        tap_two[...],
        down[...],
        state[...],
        mats,
        feeds,
        smalls_two,
        bias,
        saved_two,
        work[0],
        result_ref,
        True,
    )
    grad_now = side_backward(
        tap_two[...],
        state[...],
        cotangent[...],
        mats,
        feeds,
        smalls_two,
        bias,
        saved_two,
        work,
        partial(put_at, 1),
    )
    load(0, mats, feeds)
    grad_ref[...] = side_backward(
        tap_one[...],
        state_in[...].astype(F32),
        grad_now,
        mats,
        feeds,
        smalls_one,
        bias,
        saved_one,
        work,
        partial(put_at, 0),
    )


def side_last(places, place, tap_one, tap_two, whole, state_in, state, cotangent, smalls, bias, saved):
    tokens = state.shape[0]
    packed = places > 0
    shapes = [shape_of((tokens, S), F32)] * 2
    scratch = [pltpu.VMEM(*item) for item in saved_shapes(tokens).values()]
    scratch += [
        pltpu.VMEM((3, tokens // ROW, S, ROW), BF),
        pltpu.VMEM((3, tokens // ROW, S, ROW), F32),
        pltpu.VMEM((tokens // (2 * ROW) * TURNS, 2, 2 * ROW), F32),
    ] + MATRICES
    if packed:
        height = (L * 4 * S + L * 2 * SF + L * D) // places
        shapes += [
            shape_of((places // 2, height, S), F32),
            shape_of((places // 2, height, S), BF),
            shape_of((16, S), F32),
        ]
    else:
        shapes += [
            shape_of((L * 4 * S, S), F32),
            shape_of((L * 2 * S, SF), F32),
            shape_of((L * D, S), F32),
            shape_of((L * 3, S), F32),
        ]
    return pl.pallas_call(
        partial(side_last_kernel, packed),
        out_shape=shapes,
        in_specs=[SM] + [VM] * (8 + len(saved)),
        out_specs=[VM] * len(shapes),
        scratch_shapes=scratch,
        compiler_params=params(32),
        cost_estimate=cost(30.0),
    )(place, tap_one, tap_two, whole, state_in, state, cotangent, smalls, bias, *saved)


FAR_BIT = 6
MASKS = (1, 2, 4, 3, 5, 6, 7)


def eighths_kernel(place, kept, came, own_ref, *sent_refs):
    here = place[3] + 2 * place[4] + 4 * place[5]
    for mask, target in zip((0,) + MASKS, (own_ref,) + sent_refs):
        for last in range(2):
            spot = (here ^ mask) + 8 * last
            target[last] = (kept[spot] + came[spot].astype(F32)).astype(target.dtype)


def collect_kernel(own, *refs):
    came, (kept_ref, sent_ref) = refs[:-2], refs[-2:]
    total = own[...]
    for ref in came:
        total = total + ref[...].astype(F32)
    kept_ref[...] = total.astype(BF)
    sent_ref[...] = total.astype(BF)


def scatter_sums(place, kept, sent):
    share = (2,) + kept.shape[1:]
    devices = lax.axis_size("batch") * lax.axis_size("head")
    own, *parts = pl.pallas_call(
        eighths_kernel,
        out_shape=[shape_of(share, F32)] + [shape_of(share, BF)] * len(MASKS),
        in_specs=[SM] + [VM] * 2,
        out_specs=[VM] * (1 + len(MASKS)),
        compiler_params=params(16),
        cost_estimate=cost(0.6),
    )(place, kept, swap(sent, "head", 1))
    came = [
        lax.ppermute(part, ("batch", "head"), [(at, at ^ 2 * mask) for at in range(devices)])
        for mask, part in zip(MASKS, parts)
    ]
    kept, sent = pl.pallas_call(
        collect_kernel,
        out_shape=[shape_of(share, BF)] * 2,
        in_specs=[VM] * (1 + len(MASKS)),
        out_specs=[VM] * 2,
        compiler_params=params(16),
        cost_estimate=cost(0.6),
    )(own, *came)
    return (kept, swap(sent, "batch", 4))


def tally_kernel(place, kept, came, small, total_ref, small_ref):
    total = kept[...].astype(F32) + came[...].astype(F32)
    squares = total * total
    total_ref[...] = jnp.where(place[FAR_BIT] == 0, total[0], total[1])
    small_ref[0:8] = jnp.sum(squares.reshape(-1, 8, S), axis=0)
    small_ref[8:16] = small[8:16]


def tally(place, kept, came, small):
    return pl.pallas_call(
        tally_kernel,
        out_shape=[shape_of(kept.shape[1:], F32), shape_of((16, S), F32)],
        in_specs=[SM] + [VM] * 3,
        out_specs=[VM] * 2,
        compiler_params=params(16),
        cost_estimate=cost(0.6),
    )(place, kept, came, small)


def adamw(master, moment, square, grad_now, clip, rate, decay):
    grad_now = grad_now * clip
    moment = BETA_ONE * moment + (1.0 - BETA_ONE) * grad_now
    square = BETA_TWO * square + (1.0 - BETA_TWO) * grad_now * grad_now
    first_hat = moment / (1.0 - BETA_ONE**STEP)
    second_hat = square / (1.0 - BETA_TWO**STEP)
    master = master - rate * (first_hat / (jnp.sqrt(second_hat) + ADAM_EPS) + decay * master)
    return (master, moment, square)


def update_kernel(total, squares, *refs):
    states, (norm_ref, *outs) = refs[:12], refs[12:]
    gains = squares[8:16]
    grad_norm = jnp.sqrt(jnp.sum(squares[0:8] + gains * gains, keepdims=True))
    norm_ref[...] = grad_norm
    clip = jnp.minimum(1.0, THRESHOLD / grad_norm)
    base = 0
    for at, name in enumerate(("attend", "feed", "down", "gain")):
        master, moment, square = (ref[...] for ref in states[3 * at : 3 * at + 3])
        height, width = master.shape
        columns = []
        for _ in range(width // S):
            source = gains[:height] if name == "gain" else total[base : base + height]
            columns.append(source)
            base += height
        grad_now = columns[0] if len(columns) == 1 else jnp.concatenate(columns, axis=1)
        rate, decay = (RATE_SMALL, 0.0) if name == "gain" else (RATE_MATRIX, WEIGHT_DECAY)
        new = adamw(master, moment, square, grad_now, clip, rate, decay)
        for value, target in zip(new, outs[:3]):
            target[...] = value
        if name == "gain":
            outs = outs[3:]
        else:
            outs[3][...] = new[0].astype(BF)
            outs = outs[4:]


def update(total, squares, states):
    shapes = [shape_of((1, 1), F32)]
    for at in range(4):
        dims = states[3 * at].shape
        shapes += [shape_of(dims, F32)] * 3
        if at < 3:
            shapes.append(shape_of(dims, BF))
    return pl.pallas_call(
        update_kernel,
        out_shape=shapes,
        in_specs=[VM] * 14,
        out_specs=[VM] * len(shapes),
        compiler_params=params(16),
    )(total, squares, *states)


def swap(value, axis, bit):
    size = lax.axis_size(axis)
    return lax.ppermute(value, axis, [(at, at ^ bit) for at in range(size)])


def join(*values):
    return lax.optimization_barrier(values)


def backbone_rows(
    place,
    frozen_input,
    frozen_attend,
    frozen_output,
    frozen_expand,
    frozen_reduce,
    frozen_gains,
    attend_zero,
    bias,
    side_own,
    side_layer,
):
    rows = frozen_input.shape[0] // 4
    tokens = rows * ROW
    frozen = (frozen_attend, frozen_output, frozen_expand, frozen_reduce)
    chip_far, chip_own = split_chip(place, frozen_input)
    attend_one, attend_other, feed_zero, feed_one, feed_other = pack(place, *frozen)

    def x(value):
        return swap(value, "head", 2)

    def y(value):
        return swap(value, "batch", 1)

    def z(value):
        return swap(value, "batch", 2)

    def near(value):
        return swap(value, "head", 1)

    def double(value, came):
        return jnp.concatenate([value, came], axis=0)

    wide = shape_of((tokens, D), BF)
    sums = shape_of((tokens, D), F32)


    def attend_own(layer, normed):
        return pl.pallas_call(
            partial(attend_kernel, layer),
            out_shape=[shape_of((tokens, BLK), BF)] * 2,
            in_specs=[VM] * 4,
            out_specs=[VM] * 2,
            scratch_shapes=[pltpu.VMEM((2, 3, tokens, BLK), BF)],
            compiler_params=params(12),
            cost_estimate=cost(3.0),
        )(normed, frozen_attend, near_attend, bias)

    def attend_far(layer, normed, hidden, near_quarters, here, there, heights):
        return pl.pallas_call(
            partial(attend_far_kernel, layer),
            out_shape=[wide, wide] + [shape_of((height, D), BF) for height in heights],
            in_specs=[SM] + [VM] * 6 + [HB] * 2 + [VM] * 8,
            out_specs=[VM] * (2 + len(heights)),
            scratch_shapes=[
                pltpu.VMEM((2, 3, tokens, BLK), BF),
                pltpu.VMEM((2, tokens, BLK), BF),
                pltpu.VMEM((tokens, D), F32),
                pltpu.VMEM((tokens, D), BF),
                pltpu.VMEM((2 * BLK, D), BF),
                pltpu.SemaphoreType.DMA((2,)),
            ],
            compiler_params=params(20),
            cost_estimate=cost(6.5),
        )(
            place,
            normed,
            bias,
            hidden,
            frozen_gains,
            *near_quarters,
            frozen_output,
            near_output,
            *here,
            *there,
        )

    def finish(gain_at, hidden, total, came):
        count = 1 if gain_at is None else 2
        return pl.pallas_call(
            partial(finish_kernel, gain_at, len(came)),
            out_shape=[wide] * count,
            in_specs=[VM] * (3 + len(came)),
            out_specs=[VM] * count,
            compiler_params=params(12),
            cost_estimate=cost(1.0),
        )(hidden, total, frozen_gains, *came)

    def feed_own(layer, normed):
        return pl.pallas_call(
            partial(feed_kernel, layer, len(normed)),
            out_shape=sums,
            in_specs=[VM] * (len(normed) + 2),
            out_specs=VM,
            compiler_params=params(12),
            cost_estimate=cost(3.0),
        )(*normed, frozen_expand, frozen_reduce)

    def feed_far(sets, totals, parts, shapes):
        flat = [array for arrays in sets for array in arrays]
        outs = [shape for group in shapes for shape in group]
        return pl.pallas_call(
            partial(feed_far_kernel, [len(a) for a in sets], [len(g) for g in shapes]),
            out_shape=outs,
            in_specs=[VM] * (len(flat) + len(totals) + len(parts)),
            out_specs=[VM] * len(outs),
            compiler_params=params(16),
            cost_estimate=cost(1.0 * len(sets) * len(parts)),
        )(*flat, *totals, *parts)

    def near_all(arrays):
        return [near(array) for array in arrays]

    a0x, near_attend = x(attend_zero), near(frozen_attend)
    side = double(side_own, swap(side_own, "batch", 4))
    near_own, near_output = near(chip_own), near(frozen_output)

    a0x, near_attend, near_own, near_output, chip_far, side = join(
        a0x, near_attend, near_own, near_output, chip_far, side
    )
    far, a0y, a0z, a0x_near, side_came = x(chip_far), y(a0x), z(a0x), near(a0x), z(side)

    far, a0y, a0z, a0x_near, feed_zero = join(far, a0y, a0z, a0x_near, feed_zero)
    far_near, f0x, a0w, a0y_near = near(far), x(feed_zero), y(a0z), near(a0y)
    hidden, normed = pl.pallas_call(
        assemble_kernel,
        out_shape=[wide] * 2,
        in_specs=[SM] + [VM] * 5,
        out_specs=[VM] * 2,
        compiler_params=params(16),
        cost_estimate=cost(2.0),
    )(place, chip_own, near_own, far, far_near, frozen_gains)
    contexts = attend_own(0, normed)

    *contexts, a0w, a0y_near, a0z, side, side_came = join(
        *contexts, a0w, a0y_near, a0z, side, side_came
    )
    side = double(side, side_came)
    a0z_near, a0w_near, side_came = near(a0z), near(a0w), y(side)
    here, there = (a0x, a0y, a0z, a0w), (a0x_near, a0y_near, a0z_near, a0w_near)
    halves = split_rows(tokens, 2)
    mid, normed, *sent = attend_far(0, normed, hidden, contexts, here, there, halves)

    mid, normed, *sent, f0x, attend_one, side, side_came = join(
        mid, normed, *sent, f0x, attend_one, side, side_came
    )
    a1x, f0y, f0z, other = x(attend_one), y(f0x), z(f0x), near_all(sent)
    side = double(side, side_came)
    total = feed_own(0, [normed])
    other_total = feed_own(0, other)

    total, other_total, a1x, attend_other, side = join(
        total, other_total, a1x, attend_other, side
    )
    a1z, a1x_near, side_came = x(attend_other), near(a1x), x(side)

    f0y, f0z, a1x, a1x_near, feed_one = join(f0y, f0z, a1x, a1x_near, feed_one)
    f1x, a1y, f0w = x(feed_one), y(a1x), z(f0y)
    total, other_total = feed_far(
        ([normed], other), (total, other_total), (f0x, f0y, f0z), ([sums], [sums])
    )

    total, other_total, a1y, a1z, side, side_came = join(
        total, other_total, a1y, a1z, side, side_came
    )
    a1w, a1y_near, a1z_near = y(a1z), near(a1y), near(a1z)
    side = double(side, side_came)

    f0w, a1w, a1y_near, a1z_near = join(f0w, a1w, a1y_near, a1z_near)
    a1w_near = near(a1w)
    thirds = [shape_of((height, D), BF) for height in split_rows(tokens, 3)]
    came = near_all(feed_far([other], [other_total], [f0w], [thirds]))
    total = feed_far([[normed]], [total], [f0w], [[sums]])[0]
    hidden, normed = finish((1, 0), mid, total, came)
    taps = [hidden]
    f1x, feed_other, normed, side = join(f1x, feed_other, normed, side)
    f1w, f1y, f1z = x(feed_other), y(f1x), z(f1x)
    side = double(side, near(side))
    contexts = attend_own(1, normed)
    side_outs = side_layer(hidden, side)
    here, there = (a1x, a1y, a1z, a1w), (a1x_near, a1y_near, a1z_near, a1w_near)
    mid, normed, *sent = attend_far(1, normed, hidden, contexts, here, there, halves)
    other = near_all(sent)
    total = feed_own(1, [normed])
    other_total = feed_own(1, other)

    total, other_total, f1w, f1y, f1z, *side_outs = join(
        total, other_total, f1w, f1y, f1z, *side_outs
    )
    parts = (f1x, f1w, f1y, f1z)
    came = near_all(feed_far([other], [other_total], parts, [thirds]))
    total = feed_far([[normed]], [total], parts, [[sums]])[0]
    taps.append(finish(None, mid, total, came)[0])
    return (taps, side, side_outs)


def split_attend(normed, w_attend, w_output, same_seg):
    col_count = w_attend.shape[2]
    projected = jnp.einsum(
        "rtd,jdc->jrtc", normed, w_attend, preferred_element_type=jnp.float32
    ).astype(jnp.bfloat16)
    head_shape = normed.shape[:2] + (col_count // HEAD_DIM, HEAD_DIM)
    queries = projected[0].reshape(head_shape)
    key_rows = projected[1].reshape(head_shape)
    value_rows = projected[2].reshape(head_shape)
    scores = jnp.einsum(
        "rqhc,rkhc->rhqk", queries, key_rows, preferred_element_type=jnp.float32
    ) * HEAD_DIM ** (-0.5)
    scores = jnp.where(same_seg[:, None], scores, MASKED)
    shares = jax.nn.softmax(scores, axis=-1).astype(jnp.bfloat16)
    context = jnp.einsum("rhqk,rkhc->rqhc", shares, value_rows, preferred_element_type=jnp.float32)
    context = context.astype(jnp.bfloat16).reshape(normed.shape[:2] + (col_count,))
    return jnp.einsum("rtc,cd->rtd", context, w_output, preferred_element_type=jnp.float32)


def split_feed(normed, w_expand, w_reduce):
    inner = jax.nn.gelu(
        jnp.einsum("rtd,df->rtf", normed, w_expand, preferred_element_type=jnp.float32)
    ).astype(jnp.bfloat16)
    return jnp.einsum("rtf,fd->rtd", inner, w_reduce, preferred_element_type=jnp.float32)


def split_sublayer(hidden, gains, work):
    whole = lax.all_gather(hidden, "head", axis=2, tiled=True)
    normed = root_norm(whole.astype(jnp.float32), gains).astype(jnp.bfloat16)
    summed = lax.psum_scatter(
        work(normed).astype(jnp.bfloat16), "head", scatter_dimension=2, tiled=True
    ).astype(jnp.float32)
    return (hidden.astype(jnp.float32) + summed).astype(jnp.bfloat16)


def backbone_split(
    frozen_input, frozen_attend, frozen_output, frozen_expand, frozen_reduce, frozen_gains, lengths
):
    taps = []
    same_all, _ = segments(lengths)
    hidden = frozen_input
    for layer in range(L):
        hidden = split_sublayer(
            hidden,
            frozen_gains[layer, 0],
            partial(
                split_attend,
                w_attend=frozen_attend[layer],
                w_output=frozen_output[layer],
                same_seg=same_all,
            ),
        )
        hidden = split_sublayer(
            hidden,
            frozen_gains[layer, 1],
            partial(split_feed, w_expand=frozen_expand[layer], w_reduce=frozen_reduce[layer]),
        )
        tapped = lax.all_to_all(hidden, "head", split_axis=0, concat_axis=2, tiled=True)
        taps.append(tapped.reshape(-1, D))
    return taps


def shards(
    frozen_input,
    frozen_attend,
    frozen_output,
    frozen_expand,
    frozen_reduce,
    frozen_gains,
    lengths,
    side_input,
    cotangent,
    attend_master,
    attend_moment,
    attend_square,
    feed_master,
    feed_moment,
    feed_square,
    down_master,
    down_moment,
    down_square,
    gains_master,
    gains_moment,
    gains_square,
):
    head_count, batch_count = lax.axis_size("head"), lax.axis_size("batch")
    tuned = head_count == 4 and batch_count == 8
    head_at, batch_at = lax.axis_index("head"), lax.axis_index("batch")
    own_rows = lengths.shape[0] // head_count
    place = jnp.stack(
        [
            head_at,
            batch_at % 4,
            head_at % 2,
            head_at // 2 % 2,
            batch_at % 2,
            batch_at // 2 % 2,
            batch_at // 4 % 2,
            batch_at * head_count + head_at,
            jnp.zeros_like(head_at),
            gathered_at(batch_at * head_count + head_at) if tuned else jnp.zeros_like(head_at),
        ]
    ).astype(jnp.int32)
    tokens = own_rows * ROW
    state_in = side_input.reshape(tokens, S)
    frozen = (frozen_attend, frozen_output, frozen_expand, frozen_reduce, frozen_gains)
    masters = (attend_master, feed_master, down_master)
    given = (lengths, cotangent.reshape(tokens, S))
    if tuned:
        attend_zero = pack_first(place, frozen_attend, frozen_output)
        attend_zero, *given = join(attend_zero, *given)
    bias, grad_seed, *side_own = prepare(given[0], place, given[1], masters, tuned)
    if tuned:
        taps, whole, (*saved, state) = backbone_rows(
            place,
            frozen_input,
            *frozen,
            attend_zero,
            bias,
            *side_own,
            lambda tap, whole: side_first(place, tap, whole, state_in, gains_master, bias),
        )
    else:
        mats, feeds, downs = (
            lax.all_gather(array.astype(BF), ("batch", "head"), axis=0, tiled=True)
            for array in masters
        )
        feeds = feeds.reshape(PLACES, -1, SF // S, S).transpose(0, 2, 1, 3)
        whole = jnp.concatenate(
            [array.reshape(PLACES, -1, S) for array in (mats, feeds, downs)], axis=1
        )
        whole = whole.reshape((2,) * 5 + whole.shape[1:]).transpose(4, 3, 2, 1, 0, 5, 6)
        whole = whole.reshape(PLACES, -1, S)
        taps = backbone_split(frozen_input, *frozen, lengths)
        *saved, state = side_first(place, taps[0], whole, state_in, gains_master, bias)
    result, input_grad, *sums = side_last(
        PLACES if tuned else 0,
        place,
        *taps,
        whole,
        state_in,
        state,
        grad_seed,
        gains_master,
        bias,
        saved,
    )
    result = result.reshape(cotangent.shape)
    input_grad = input_grad.reshape(cotangent.shape)
    states = (
        attend_master,
        attend_moment,
        attend_square,
        feed_master,
        feed_moment,
        feed_square,
        down_master,
        down_moment,
        down_square,
        gains_master,
        gains_moment,
        gains_square,
    )
    if tuned:
        kept, sent, small = sums
        small = small + swap(small, "batch", 4)
        kept, came = scatter_sums(place, kept, sent)
        total, small = tally(place, kept, came, small)
        for bit in (1, 2):
            small = small + swap(small, "head", bit)
        by_y, by_z, by_both = (swap(small, "batch", bit) for bit in (1, 2, 3))
        small = (small + by_y) + (by_z + by_both)
        grad_norm, *rest = update(total, small, states)
        return (result, input_grad, grad_norm.reshape(()), *rest)
    grads = lax.psum(tuple(sums), ("batch", "head"))
    grad_norm = jnp.sqrt(sum(jnp.sum(grad * grad) for grad in grads))
    clip = jnp.minimum(1.0, THRESHOLD / grad_norm)
    member = lax.axis_index(("batch", "head"))
    outs = []
    for at, grad in enumerate(grads):
        owned = states[3 * at : 3 * at + 3]
        if at < 3:
            height = owned[0].shape[0]
            grad = lax.dynamic_slice_in_dim(grad, member * height, height, 0)
        rate, decay = (RATE_MATRIX, WEIGHT_DECAY) if at < 3 else (RATE_SMALL, 0.0)
        new = adamw(*owned, grad, clip, rate, decay)
        outs.extend(new)
        if at < 3:
            outs.append(new[0].astype(BF))
    return (result, input_grad, grad_norm, *outs)


def solution(mesh):
    row_split = P(("batch", "head"), None)
    cube_split = P(("batch", "head"), None, None)
    return jax.shard_map(
        shards,
        mesh=mesh,
        in_specs=(
            P("batch", None, "head"),
            P(None, None, None, "head"),
            P(None, "head", None),
            P(None, None, "head"),
            P(None, "head", None),
            P(),
            P("batch", None),
            cube_split,
            cube_split,
        )
        + (row_split,) * 9
        + (P(),) * 3,
        out_specs=(cube_split, cube_split, P()) + (row_split,) * 12 + (P(),) * 3,
        check_vma=False,
    )
```
